512 devices in a mesh: section: 4 (over x), dp: 32 (over z, y_hi), mp: 4 (over y_lo, core).
Axes of the slice: x: 4, y: 4 (y_hi: 2, y_lo: 2; y = y_hi * 2 + y_lo), z: 16, core: 2. Of those that a mesh axis runs over, the one named last changes fastest.
Arguments:
- patches: bfloat16 [6144, 3200], P('dp', ('section', 'mp')), may hold values from -6 to 6
- up_first: bfloat16 [3200, 6400], P('dp', ('section', 'mp')), may hold values from -0.109375 to 0.109375
- down_first: bfloat16 [6400, 3200], P(('section', 'mp'), 'dp'), may hold values from -0.078125 to 0.078125
- up_second: bfloat16 [3200, 6400], P('dp', ('section', 'mp')), may hold values from -0.109375 to 0.109375
- down_second: bfloat16 [6400, 3200], P(('section', 'mp'), 'dp'), may hold values from -0.078125 to 0.078125
- targets: int32 [6144, 1], P('dp'), may hold values from 0 to 31; in each aligned block of 192 rows (0 to 191, 192 to 383, ...) at most 12 rows name the same one
Outputs:
- placed: bfloat16 [12288, 3200], P('dp', ('section', 'mp'))
The draws below stay inside these ranges and needn't reach their ends.
Inputs may be any that keep to these rules, and one draw needn't show every extreme that they name: `targets`: of the rows of one block of 192, at most 12 have the same target, a bound that some block reaches.
All inputs are finite; a program needn't handle non-finite values.
Results may differ from the reference program's by a relative error of at most 0.022.
Values may be sent and summed in bfloat16 or wider, within the bound.
A program may use at most 64 MiB of HBM per device.

```python
import math
import jax
import jax.numpy as jnp
import numpy as np
from jax import lax

DV = 3200
FV = 6400
ROWS_DEV = 192
NV = 6144
CAP = 12
SLOTS = 12288
N_SECTION = 4
N_DP = 32
N_MP = 4


def shard_levels(stream_key, extent, cuts, least, largest):
    def one(axis_at, shards_of):
        draws = jax.random.uniform(jax.random.fold_in(jax.random.fold_in(stream_key, 6), axis_at), (shards_of,), jnp.float32, least / len(cuts), largest / len(cuts))
        return jnp.repeat(jnp.exp(draws), extent[axis_at] // shards_of).reshape((-1,) + (1,) * (len(extent) - axis_at - 1))

    gain = one(*cuts[0])
    for cut in cuts[1:]:
        gain = gain * one(*cut)
    return gain


def shared_out(own_key, own, number, rows, number_of, top, most, lean):
    ranking = jax.random.permutation(own_key, number_of)
    crowded, usual = load_shares(number_of, rows * top, most, lean, True), load_shares(number_of, rows * top, most, lean, False)
    places = jnp.arange(number_of)

    def named(tallies, rotation):
        used = int((tallies > 0).sum())
        fixed = max(1, used // 4)
        moved = fixed + (places - fixed + rotation * (used - fixed)) % max(1, number_of - fixed)
        return jnp.zeros((number_of,), jnp.int32).at[ranking[jnp.where(places < fixed, places, moved)]].set(jnp.asarray(tallies, jnp.int32))

    tallies = jnp.where(number % 4 == 0, named(crowded, number // 4), named(usual, number - number // 4 - 1))
    mixed = jax.random.permutation(jax.random.fold_in(own, 3), number_of)
    donor, taker = mixed[0:number_of // 2 * 2:2], mixed[1:number_of // 2 * 2:2]
    slack = jnp.minimum(tallies[donor] - 1, most - tallies[taker]) // 2
    slack = jnp.where((donor == ranking[0]) | (taker == ranking[0]) | (tallies[taker] == 0), 0, jnp.maximum(slack, 0))
    moved = jax.random.randint(jax.random.fold_in(own, 4), (number_of // 2,), 0, 1 << 20) % (slack + 1)
    tallies = tallies.at[donor].add(-moved).at[taker].add(moved)
    items = jnp.searchsorted(jnp.cumsum(tallies), jnp.arange(rows * top), side="right").astype(jnp.int32)
    table = items.reshape(top, rows).T
    table = table[jax.random.permutation(jax.random.fold_in(own, 1), rows)]
    rotation = jax.random.randint(jax.random.fold_in(own, 2), (rows, 1), 0, top)
    return jnp.take_along_axis(table, (jnp.arange(top)[None, :] + rotation) % top, axis=1)


def load_shares(number_of, total, limit, slope, full):
    portions = [(1 << 20) // math.isqrt(grade ** slope) + 1 for grade in range(1, number_of + 1)]
    largest = limit if full else min(limit, max(-(-total // number_of), total * portions[0] // sum(portions)))
    least = 1 if total - largest >= number_of - 1 else 0
    counts, rest = [largest] + [least] * (number_of - 1), total - largest - least * (number_of - 1)
    while rest > 0:
        candidates = [i for i in range(1, number_of) if counts[i] < largest] or [i for i in range(1, number_of) if counts[i] < limit]
        whole, budget = sum([portions[i] for i in candidates]), rest
        for i in candidates:
            extra = min(limit - counts[i], max(1, budget * portions[i] // whole), rest)
            counts[i] = counts[i] + extra
            rest = rest - extra
    return np.array(counts)


def scatter_about(rng, shape, scale, bound, pieces=(), kind=jnp.bfloat16):
    gain = shard_levels(rng, shape, pieces, -0.22, 0.18) if pieces else 1.0
    result = jax.random.normal(rng, shape, jnp.float32) * scale * gain
    return jnp.minimum(jnp.maximum(result, -bound), bound).astype(kind)


def setup_inputs(seed: int = 0) -> dict:
    keys = jax.random.split(jax.random.key(seed), 7)
    patches = scatter_about(keys[0], (NV, DV), 1.0, 6.0, ((0, 32), (1, 16)))
    up_first = scatter_about(keys[1], (DV, FV), DV ** -0.5, 0.109375, ((0, 32), (1, 16)))
    down_first = scatter_about(keys[2], (FV, DV), FV ** -0.5, 0.078125, ((0, 16), (1, 32)))
    up_second = scatter_about(keys[3], (DV, FV), DV ** -0.5, 0.109375, ((0, 32), (1, 16)))
    down_second = scatter_about(keys[4], (FV, DV), FV ** -0.5, 0.078125, ((0, 16), (1, 32)))
    targets_keys = jax.random.split(jax.random.fold_in(keys[5], 1), NV // ROWS_DEV)
    targets_turns = jax.random.permutation(jax.random.fold_in(keys[5], 3), NV // ROWS_DEV)
    targets = jax.vmap(lambda own, number: shared_out(jax.random.fold_in(keys[5], 2), own, number, ROWS_DEV, N_DP, 1, CAP, 2))(targets_keys, targets_turns).reshape((NV, 1))
    return dict(patches=patches, up_first=up_first, down_first=down_first, up_second=up_second, down_second=down_second, targets=targets)


epsilon = 1e-06

def layer(rows, up_weight, down_weight):
    floated = rows.astype(jnp.float32)
    scale = lax.rsqrt(lax.optimization_barrier(jnp.mean(floated * floated, axis=-1, keepdims=True)) + epsilon)
    normed = (floated * scale).astype(jnp.bfloat16)
    hidden = jax.nn.gelu(jnp.dot(normed, up_weight, preferred_element_type=jnp.float32)).astype(jnp.bfloat16)
    groups = N_SECTION * N_MP
    width = FV // groups
    total = jnp.zeros(floated.shape, jnp.float32)
    for group in range(groups):
        partial_sum = jnp.dot(hidden[:, group * width:(group + 1) * width], down_weight[group * width:(group + 1) * width], preferred_element_type=jnp.float32)
        rounded = lax.optimization_barrier(partial_sum.astype(jnp.bfloat16))
        total = total + rounded.astype(jnp.float32)
    return (floated + total).astype(jnp.bfloat16)

def reference(patches, up_first, down_first, up_second, down_second, targets):
    first = layer(patches, up_first, down_first)
    second = layer(first, up_second, down_second)
    route_table = targets[:, 0].reshape(N_DP, ROWS_DEV)
    onehot = (route_table[:, :, None] == jnp.arange(N_DP, dtype=jnp.int32)[None, None, :]).astype(jnp.int32)
    position = lax.optimization_barrier(jnp.sum(jnp.cumsum(onehot, axis=1) * onehot, axis=2)) - 1
    source = jnp.arange(N_DP, dtype=jnp.int32)[:, None]
    slots = (route_table * (N_DP * CAP) + source * CAP + position).reshape(-1).astype(jnp.int32)
    return jnp.zeros((SLOTS, DV), jnp.bfloat16).at[slots].set(second)
```

```python
import functools

import jax
import jax.numpy as jnp
from jax import lax
from jax.experimental import pallas as pl
from jax.experimental.pallas import tpu as pltpu
from jax.sharding import PartitionSpec as P

MESH = pl.DeviceIdType.MESH
EPSILON = 1e-06
DV = 3200
ROWS = 192
NZ = 16
HALF = 100
PACK = 352
CHUNKS = 2
CHUNK = PACK // CHUNKS
LANES = 256
STAGGER = 6
CAP = 12
SLOT = 16


def remote(src, dst, send, recv, device):
    return pltpu.make_async_remote_copy(
        src_ref=src, dst_ref=dst, send_sem=send, recv_sem=recv, device_id=device, device_id_type=MESH
    )


def weight_tiles(first, second):
    gap = jnp.zeros((16, 384), jnp.bfloat16)

    def wide(block):
        return jnp.concatenate([block[112 * j : 112 * j + 112] for j in range(3)], axis=1)

    main = jnp.concatenate([wide(first), gap, wide(second), gap], axis=0)
    rest = jnp.concatenate([first[336:352], second[336:352]], axis=1)
    return main, rest


def dot(a, b):
    return jnp.dot(a, b, preferred_element_type=jnp.float32)


def dot_nt(a, b):
    return lax.dot_general(a, b, (((1,), (1,)), ((), ())), preferred_element_type=jnp.float32)


def kernel(
    x_ref, w_ref, trow_ref, tcol_ref, out_ref,
    weights, xs, acc, acc_rest, squares, hid, hid_rest, staged, first_sum, staged_sum, second_sum, mine,
    pick, outbox, inbox,
    swap_send, swap_recv, ring_up_send, ring_down_send, ring_recv, sib_send, sib_recv,
    gather_send, gather_recv, one_send, one_recv, two_send, two_recv, route_send, route_recv,
):
    x, dp, mp = lax.axis_index("section"), lax.axis_index("dp"), lax.axis_index("mp")
    z, yh, yl, c = dp // 2, dp % 2, mp // 2, mp % 2
    y = yh * 2 + yl
    group = x * 4 + mp

    def at(xx, zz, yy, cc):
        return {"section": xx, "dp": zz * 2 + yy // 2, "mp": (yy % 2) * 2 + cc}

    up, down = at(x, (z + 1) % NZ, y, c), at(x, (z + NZ - 1) % NZ, y, c)
    sibling = at(x, z, y, 1 - c)
    partner = at(x, z, (1 - yh) * 2 + yl, 1 - c)

    barrier = pltpu.get_barrier_semaphore()

    def greet_plane(i, _):
        dx, dy, dc = i // 8, (i // 2) % 4, i % 2
        pl.semaphore_signal(
            barrier, inc=1, device_id=at((x + dx) % 4, z, (y + dy) % 4, (c + dc) % 2), device_id_type=MESH
        )
        return 0

    def greet_line(i, _):
        dz, dh = i // 2, i % 2
        pl.semaphore_signal(
            barrier, inc=1, device_id={"dp": ((z + dz) % NZ) * 2 + (yh + dh) % 2}, device_id_type=MESH
        )
        return 0

    lax.fori_loop(1, 32, greet_plane, 0)
    lax.fori_loop(2, 32, greet_line, 0)

    trow, tcol = trow_ref[...], tcol_ref[...]
    before = lax.broadcasted_iota(jnp.int32, (ROWS, ROWS), 0) < lax.broadcasted_iota(jnp.int32, (ROWS, ROWS), 1)
    same = jnp.where(jnp.logical_and(before, tcol == trow), 1.0, 0.0)
    slot = trow * SLOT + jnp.sum(same, axis=0, keepdims=True).astype(jnp.int32)
    pick[...] = jnp.where(
        lax.broadcasted_iota(jnp.int32, (32 * SLOT, ROWS), 0) == slot, 1.0, 0.0
    ).astype(jnp.bfloat16)

    pl.semaphore_wait(barrier, 61)

    own = z * 2 + c

    def chunk(m, s, ch):
        return weights.at[m, s, pl.ds(ch * CHUNK, CHUNK)]

    def swap_copy(m):
        return remote(w_ref.at[m], weights.at[m, z * 2 + 1 - c], swap_send.at[m], swap_recv.at[m], partner)

    def up_copy(m, zz, ch):
        return remote(
            chunk(m, zz * 2 + c, ch), chunk(m, zz * 2 + c, ch), ring_up_send.at[m, zz, ch], ring_recv.at[m, zz, ch], up
        )

    def down_copy(m, zz, ch):
        return remote(
            chunk(m, zz * 2 + c, ch), chunk(m, zz * 2 + c, ch), ring_down_send.at[m, zz, ch], ring_recv.at[m, zz, ch], down
        )

    def sib_copy(m, zz, cc):
        return remote(
            weights.at[m, zz * 2 + cc], weights.at[m, zz * 2 + cc], sib_send.at[m, zz], sib_recv.at[m, zz], sibling
        )

    def swap_start():
        @pl.when(yh != c)
        def _():
            for m in range(4):
                swap_copy(m).start()

        @pl.when(yh == c)
        def _():
            for m in range(4):
                weights[m, own] = w_ref[m]

    def ring_start(m):
        @pl.when(yh != c)
        def _():
            swap_copy(m).wait_recv()

        for ch in range(CHUNKS):
            up_copy(m, z, ch).start()
            down_copy(m, z, ch).start()
        sib_copy(m, z, c).start()

    def ring_tick(m, s):
        a, b = (z + NZ - s) % NZ, (z + s) % NZ
        for ch in range(CHUNKS):
            up_copy(m, a, ch).wait_recv()

            @pl.when((s < 7) | ((s == 7) & (ch == 0)))
            def _(ch=ch):
                up_copy(m, a, ch).start()

            @pl.when(s < 8)
            def _(ch=ch):
                down_copy(m, b, ch).wait_recv()

            @pl.when((s < 7) | ((s == 7) & (ch == 1)))
            def _(ch=ch):
                down_copy(m, b, ch).start()

        sib_copy(m, a, c).start()

        @pl.when(s < 8)
        def _():
            sib_copy(m, b, c).start()

    def ticks(low, high, work=None):
        def body(t, _):
            for m in range(4):
                s = t - STAGGER * m

                if low - STAGGER * m > 8 or high - STAGGER * m < 1:
                    continue

                @pl.when((s >= 1) & (s <= 8))
                def _(m=m, s=s):
                    ring_tick(m, s)

                if m < 3:

                    @pl.when(t == STAGGER * (m + 1))
                    def _(m=m):
                        ring_start(m + 1)

            if work is not None:
                work(t)
            return 0

        lax.fori_loop(low, high + 1, body, 0)

    def gather_copy(layer, i, g):
        dx, dy = i // 4, i % 4
        return remote(
            mine.at[layer], xs.at[layer, g], gather_send.at[layer, i], gather_recv.at[layer, g],
            at((x + dx) % 4, z, (y + dy) % 4, yh),
        )

    def gather_start(layer):
        def body(i, _):
            gather_copy(layer, i, group).start()
            return 0

        lax.fori_loop(1, 16, body, 0)

        @pl.when(c != yh)
        def _():
            gather_copy(layer, 0, group).start()

        @pl.when(c == yh)
        def _():
            xs[layer, group] = mine[layer]

    def gather_wait(layer, g):
        @pl.when((g != group) | (yh != c))
        def _():
            gather_copy(layer, 1, g).wait_recv()

    def begin_up():
        acc[...] = jnp.zeros_like(acc)
        acc_rest[...] = jnp.zeros_like(acc_rest)
        squares[...] = jnp.zeros_like(squares)

    def up_unit(layer, zz):
        m = 2 * layer
        gather_wait(layer, zz)
        sib_copy(m, zz, 1 - c).wait_recv()
        main, rest = weight_tiles(weights[m, zz * 2], weights[m, zz * 2 + 1])
        rows = xs[layer, zz]
        acc[...] += dot(rows, main)
        acc_rest[...] += dot_nt(rows, rest)
        wide = rows.astype(jnp.float32)
        wide = wide * wide
        squares[...] += wide[:, :128] + wide[:, 128:]

    def end_up():
        scale = lax.rsqrt(jnp.sum(squares[...], axis=1, keepdims=True) * (1.0 / DV) + EPSILON)

        def act(v):
            v = v * scale
            return (0.5 * v * (1.0 + jnp.tanh(0.7978845608028654 * (v + 0.044715 * (v * v * v))))).astype(jnp.bfloat16)

        hid[...] = act(acc[...])
        hid_rest[...] = act(acc_rest[...])

    def one_copy(layer, zz, yy):
        return remote(
            staged.at[layer, zz], first_sum.at[layer, zz // 4, yy], one_send.at[layer, zz], one_recv.at[layer, zz // 4, yy],
            at(x, z, c * 2 + (zz // 2) % 2, zz % 2),
        )

    def to_self(zz):
        return (yh == c) & ((zz // 2) % 2 == yl) & (zz % 2 == c)

    def down_unit(layer, zz):
        m = 2 * layer + 1
        sib_copy(m, zz, 1 - c).wait_recv()
        main, rest = weight_tiles(weights[m, zz * 2], weights[m, zz * 2 + 1])
        part = (dot_nt(hid[...], main) + dot(hid_rest[...], rest)).astype(jnp.bfloat16)

        @pl.when(to_self(zz))
        def _():
            first_sum[layer, zz // 4, y] = part

        @pl.when(jnp.logical_not(to_self(zz)))
        def _():
            staged[layer, zz] = part
            one_copy(layer, zz, y).start()

    def two_copy(layer, xx, src):
        return remote(
            staged_sum.at[layer, xx], second_sum.at[layer, src], two_send.at[layer, xx], two_recv.at[layer, src],
            at(xx, z, y, c),
        )

    def collect(layer):
        def body(i, _):
            xx = (x + i) % 4
            total = None
            for yy in range(4):

                @pl.when((yy != y) | (yh != c))
                def _(yy=yy):
                    one_copy(layer, xx * 4, yy).wait_recv()

                part = first_sum[layer, xx, yy].astype(jnp.float32)
                total = part if total is None else total + part
            total = total.astype(jnp.bfloat16)

            @pl.when(xx == x)
            def _():
                second_sum[layer, x] = total

            @pl.when(xx != x)
            def _():
                staged_sum[layer, xx] = total
                two_copy(layer, xx, x).start()

            return 0

        lax.fori_loop(0, 4, body, 0)

    def own_total(layer):
        total = mine[layer].astype(jnp.float32)
        for xx in range(4):

            @pl.when(xx != x)
            def _(xx=xx):
                two_copy(layer, x, xx).wait_recv()

            total = total + second_sum[layer, xx].astype(jnp.float32)
        return total.astype(jnp.bfloat16)

    def units(run, low, high):
        def body(i, _):
            d = (i + 1) // 2
            run((z + jnp.where(i % 2 == 1, d, NZ - d)) % NZ)
            return 0

        lax.fori_loop(low, high, body, 0)

    swap_start()
    mine[0] = x_ref[...]
    ring_start(0)
    gather_start(0)
    begin_up()
    ticks(1, 7)
    ticks(8, 11, lambda t: units(functools.partial(up_unit, 0), (t - 8) * 4, (t - 8) * 4 + 4))
    end_up()
    ticks(12, 15, lambda t: units(functools.partial(down_unit, 0), (t - 12) * 4, (t - 12) * 4 + 4))
    begin_up()
    ticks(16, 17)
    collect(0)
    ticks(18, 18)
    mine[1] = own_total(0)
    gather_start(1)
    ticks(19, 26)
    units(functools.partial(up_unit, 1), 0, 16)
    end_up()
    units(functools.partial(down_unit, 1), 0, 16)
    collect(1)
    second = own_total(1)
    outbox[...] = dot(pick[...], second).astype(jnp.bfloat16).reshape(32, SLOT, LANES)

    def route_copy(d, s):
        return remote(outbox.at[d], inbox.at[s], route_send.at[d], route_recv.at[s], {"dp": d})

    def route_start(i, _):
        route_copy((dp + i) % 32, dp).start()
        return 0

    lax.fori_loop(1, 32, route_start, 0)
    inbox[dp] = outbox[dp]

    @pl.when(yh != c)
    def _():
        for m in range(4):
            swap_copy(m).wait_send()

    def drain_ring(i, _):
        m, s = i // 9, i % 9
        a, b = (z + NZ - s) % NZ, (z + s) % NZ
        for ch in range(CHUNKS):

            @pl.when((s < 7) | ((s == 7) & (ch == 0)))
            def _(ch=ch):
                up_copy(m, a, ch).wait_send()

            @pl.when((s < 7) | ((s == 7) & (ch == 1)))
            def _(ch=ch):
                down_copy(m, b, ch).wait_send()

        sib_copy(m, a, c).wait_send()

        @pl.when((s > 0) & (s < 8))
        def _():
            sib_copy(m, b, c).wait_send()

        return 0

    lax.fori_loop(0, 36, drain_ring, 0)
    for layer in range(2):

        def drain_gather(i, _, layer=layer):
            gather_copy(layer, i, group).wait_send()
            return 0

        lax.fori_loop(1, 16, drain_gather, 0)

        @pl.when(c != yh)
        def _(layer=layer):
            gather_copy(layer, 0, group).wait_send()

        def drain_one(zz, _, layer=layer):
            @pl.when(jnp.logical_not(to_self(zz)))
            def _():
                one_copy(layer, zz, y).wait_send()

            return 0

        lax.fori_loop(0, 16, drain_one, 0)

        def drain_two(i, _, layer=layer):
            two_copy(layer, (x + i) % 4, x).wait_send()
            return 0

        lax.fori_loop(1, 4, drain_two, 0)

    def route_wait(i, _):
        route_copy((dp + i) % 32, (dp + i) % 32).wait()
        return 0

    lax.fori_loop(1, 32, route_wait, 0)
    r = lax.broadcasted_iota(jnp.int32, (32 * CAP, 32 * SLOT), 0)
    q = lax.broadcasted_iota(jnp.int32, (32 * CAP, 32 * SLOT), 1)
    squeeze = jnp.where(((q & 15) < CAP) & (r == (q >> 4) * CAP + (q & 15)), 1.0, 0.0).astype(jnp.bfloat16)
    out_ref[...] = dot(squeeze, inbox[...].reshape(32 * SLOT, LANES)).astype(jnp.bfloat16)


def pack(w):
    main = jnp.pad(w[:, :384], ((0, 12), (0, 0))).reshape(112, 3, 128).transpose(1, 0, 2).reshape(336, 128)
    return jnp.concatenate([main, jnp.pad(w[:, 384:].T, ((0, 0), (0, 28)))], axis=0)


def on_device(patches, up_first, down_first, up_second, down_second, targets):
    rows = jnp.pad(patches.reshape(ROWS, 2, HALF), ((0, 0), (0, 0), (0, 28))).reshape(ROWS, LANES)
    packed = jnp.stack([pack(up_first), pack(down_first.T), pack(up_second), pack(down_second.T)])
    bf16, dma = jnp.bfloat16, pltpu.SemaphoreType.DMA
    vmem = pl.BlockSpec(memory_space=pltpu.VMEM)
    placed = pl.pallas_call(
        kernel,
        out_shape=jax.ShapeDtypeStruct((32 * CAP, LANES), bf16),
        in_specs=[vmem] * 4,
        out_specs=vmem,
        scratch_shapes=[
            pltpu.VMEM((4, 32, PACK, 128), bf16),
            pltpu.VMEM((2, 16, ROWS, LANES), bf16),
            pltpu.VMEM((ROWS, 384), jnp.float32),
            pltpu.VMEM((ROWS, 16), jnp.float32),
            pltpu.VMEM((ROWS, 128), jnp.float32),
            pltpu.VMEM((ROWS, 384), bf16),
            pltpu.VMEM((ROWS, 16), bf16),
            pltpu.VMEM((2, 16, ROWS, LANES), bf16),
            pltpu.VMEM((2, 4, 4, ROWS, LANES), bf16),
            pltpu.VMEM((2, 4, ROWS, LANES), bf16),
            pltpu.VMEM((2, 4, ROWS, LANES), bf16),
            pltpu.VMEM((2, ROWS, LANES), bf16),
            pltpu.VMEM((32 * SLOT, ROWS), bf16),
            pltpu.VMEM((32, SLOT, LANES), bf16),
            pltpu.VMEM((32, SLOT, LANES), bf16),
            dma((4,)), dma((4,)),
            dma((4, NZ, CHUNKS)), dma((4, NZ, CHUNKS)), dma((4, NZ, CHUNKS)),
            dma((4, NZ)), dma((4, NZ)),
            dma((2, 16)), dma((2, 16)),
            dma((2, 16)), dma((2, 4, 4)),
            dma((2, 4)), dma((2, 4)),
            dma((32,)), dma((32,)),
        ],
        compiler_params=pltpu.CompilerParams(
            collective_id=0, has_side_effects=True, vmem_limit_bytes=48 * 1024 * 1024
        ),
    )(rows, packed, targets.reshape(1, ROWS), targets)
    return placed.reshape(32 * CAP, 2, 128)[:, :, :HALF].reshape(32 * CAP, 2 * HALF)


def solution(mesh):
    in_specs = (
        P("dp", ("section", "mp")),
        P("dp", ("section", "mp")),
        P(("section", "mp"), "dp"),
        P("dp", ("section", "mp")),
        P(("section", "mp"), "dp"),
        P("dp", None),
    )
    return jax.shard_map(
        on_device, mesh=mesh, in_specs=in_specs, out_specs=P("dp", ("section", "mp")), check_vma=False
    )
```

```python
import functools

import jax
import jax.numpy as jnp
from jax import lax
from jax.experimental import pallas as pl
from jax.experimental.pallas import tpu as pltpu
from jax.sharding import PartitionSpec as P

MESH = pl.DeviceIdType.MESH
EPSILON = 1e-06
DV = 3200
ROWS = 192
NZ = 16
HALF = 100
PACK = 320
CHUNKS = 2
CHUNK = PACK // CHUNKS
LANES = 256
OFFSETS = (0, 0, 4, 4)
LAST = 12
CAP = 12
SLOT = 16


def remote(src, dst, send, recv, device):
    return pltpu.make_async_remote_copy(
        src_ref=src, dst_ref=dst, send_sem=send, recv_sem=recv, device_id=device, device_id_type=MESH
    )


def one_hot(mask):
    return jnp.where(mask, 1.0, 0.0).astype(jnp.bfloat16)


def iota(shape, axis):
    return lax.broadcasted_iota(jnp.int32, shape, axis)


def pack(block):
    turned = dot_nt(one_hot(iota((HALF, HALF), 0) == iota((HALF, HALF), 1)), block[0:384])
    tiles = [turned[:, 128 * j : 128 * j + 128] for j in range(3)]
    ends = jnp.concatenate([tile[96:100] for tile in tiles] + [jnp.zeros((4, 128), jnp.float32)], axis=0)
    return jnp.concatenate([tile[0:96].astype(jnp.bfloat16) for tile in tiles] + [ends.astype(jnp.bfloat16)], axis=0)


def weight_tiles(first, second):
    gap = jnp.zeros((16, 384), jnp.bfloat16)

    def wide(block):
        ends = block[288:304].astype(jnp.float32)
        none = jnp.zeros((12, 128), jnp.float32)
        ends = [jnp.concatenate([ends[4 * j : 4 * j + 4], none], axis=0).astype(jnp.bfloat16) for j in range(3)]
        return [jnp.concatenate([block[96 * j : 96 * j + 96] for j in range(3)], axis=1), jnp.concatenate(ends, axis=1), gap]

    main = jnp.concatenate(wide(first) + wide(second), axis=0)
    rest = jnp.concatenate([first[304:320], second[304:320]], axis=1)
    return main, rest


def dot(a, b):
    return jnp.dot(a, b, preferred_element_type=jnp.float32)


def dot_nt(a, b):
    return lax.dot_general(a, b, (((1,), (1,)), ((), ())), preferred_element_type=jnp.float32)


def kernel(
    x_hbm, w0_hbm, w1_hbm, w2_hbm, w3_hbm, trow_ref, out_ref,
    x_ref, w_ref, packed, load_sem, weights, xs, acc, acc_rest, squares, hid, hid_rest, staged, first_sum, staged_sum, second_sum, mine,
    pick, squeeze, outbox, inbox,
    swap_send, swap_recv, ring_up_send, ring_down_send, ring_recv, sib_send, sib_recv,
    gather_send, gather_recv, pass_y_send, pass_x_send, one_send, one_recv, two_send, two_recv, route_send, route_recv,
):
    x, dp, mp = lax.axis_index("section"), lax.axis_index("dp"), lax.axis_index("mp")
    z, yh, yl, c = dp // 2, dp % 2, mp // 2, mp % 2
    y = yh * 2 + yl
    group = x * 4 + mp

    def at(xx, zz, yy, cc):
        return {"section": xx, "dp": zz * 2 + yy // 2, "mp": (yy % 2) * 2 + cc}

    up, down = at(x, (z + 1) % NZ, y, c), at(x, (z + NZ - 1) % NZ, y, c)
    sibling = at(x, z, y, 1 - c)
    lane_y, lane_c = c * 2 + yl, yh
    lane, lane_sibling = at(x, z, lane_y, lane_c), at(x, z, lane_y, 1 - lane_c)
    lane_up, lane_down = at(x, (z + 1) % NZ, lane_y, lane_c), at(x, (z + NZ - 1) % NZ, lane_y, lane_c)

    barrier = pltpu.get_barrier_semaphore()

    def greet_plane(i, _):
        dx, dy, dc = i // 8, (i // 2) % 4, i % 2
        pl.semaphore_signal(
            barrier, inc=1, device_id=at((x + dx) % 4, z, (y + dy) % 4, (c + dc) % 2), device_id_type=MESH
        )
        return 0

    lax.fori_loop(1, 32, greet_plane, 0)
    for device in (up, down, lane_up, lane_down):
        pl.semaphore_signal(barrier, inc=1, device_id=device, device_id_type=MESH)

    loads = [pltpu.make_async_copy(x_hbm, x_ref, load_sem.at[4])]
    loads += [
        pltpu.make_async_copy(ref, w_ref.at[m], load_sem.at[m]) for m, ref in enumerate((w0_hbm, w1_hbm, w2_hbm, w3_hbm))
    ]
    for load in loads:
        load.start()

    trow = trow_ref[...]
    named = jnp.where(iota((32, ROWS), 0) == trow, 1.0, 0.0)
    before = one_hot(iota((ROWS, ROWS), 0) < iota((ROWS, ROWS), 1))
    position = jnp.sum(named * dot(named.astype(jnp.bfloat16), before), axis=0, keepdims=True).astype(jnp.int32)
    pick[...] = one_hot(iota((32 * SLOT, ROWS), 0) == trow * SLOT + position)

    for m in range(4):
        loads[1 + m].wait()
        packed[m, 0:304] = pack(w_ref[m])
        packed[m, 304:320] = jnp.zeros((16, 128), jnp.bfloat16)
        packed[m, 304:320, 0:HALF] = w_ref[m, 384:400]
    loads[0].wait()
    widen = one_hot(iota((2 * HALF, LANES), 1) == iota((2 * HALF, LANES), 0) + jnp.where(iota((2 * HALF, LANES), 0) < HALF, 0, 28))
    mine[0] = dot(x_ref[...], widen).astype(jnp.bfloat16)

    pl.semaphore_wait(barrier, 35)

    def chunk(m, s, ch):
        return weights.at[m, s, pl.ds(ch * CHUNK, CHUNK)]

    def up_copy(m, zz, ch):
        return remote(
            chunk(m, zz * 2 + c, ch), chunk(m, zz * 2 + c, ch), ring_up_send.at[m, zz, ch], ring_recv.at[m, zz, ch], up
        )

    def down_copy(m, zz, ch):
        return remote(
            chunk(m, zz * 2 + c, ch), chunk(m, zz * 2 + c, ch), ring_down_send.at[m, zz, ch], ring_recv.at[m, zz, ch], down
        )

    def sib_copy(m, zz, cc):
        return remote(
            weights.at[m, zz * 2 + cc], weights.at[m, zz * 2 + cc], sib_send.at[m, zz], sib_recv.at[m, zz], sibling
        )

    def start_copies(m):
        slot = z * 2 + lane_c
        copies = []
        for ch in range(CHUNKS):
            src, dst = packed.at[m, pl.ds(ch * CHUNK, CHUNK)], chunk(m, slot, ch)
            copies.append(remote(src, dst, ring_up_send.at[m, z, ch], ring_recv.at[m, z, ch], lane_up))
            copies.append(remote(src, dst, ring_down_send.at[m, z, ch], ring_recv.at[m, z, ch], lane_down))
        copies.append(remote(packed.at[m], weights.at[m, slot], sib_send.at[m, z], sib_recv.at[m, z], lane_sibling))
        return copies

    def lane_copy(m):
        return remote(packed.at[m], weights.at[m, z * 2 + lane_c], swap_send.at[m], swap_recv.at[m], lane)

    def ring_start(m):
        for copy in start_copies(m):
            copy.start()

        @pl.when(yh != c)
        def _():
            lane_copy(m).start()

        @pl.when(yh == c)
        def _():
            weights[m, z * 2 + c] = packed[m]

    def weights_wait(m, zz):
        sib_copy(m, zz, 1 - c).wait_recv()

        @pl.when((zz == z) & (yh != c))
        def _():
            lane_copy(m).wait_recv()

    def ring_tick(m, s):
        a, b = (z + NZ - s) % NZ, (z + s) % NZ
        for ch in range(CHUNKS):
            up_copy(m, a, ch).wait_recv()

            @pl.when((s < 7) | ((s == 7) & (ch == 0)))
            def _(ch=ch):
                up_copy(m, a, ch).start()

            @pl.when(s < 8)
            def _(ch=ch):
                down_copy(m, b, ch).wait_recv()

            @pl.when((s < 7) | ((s == 7) & (ch == 1)))
            def _(ch=ch):
                down_copy(m, b, ch).start()

        sib_copy(m, a, c).start()

        @pl.when(s < 8)
        def _():
            sib_copy(m, b, c).start()

    def ticks(low, high, work=None):
        def body(t, _):
            for m in range(4):
                if OFFSETS[m] and low <= OFFSETS[m] + 1 <= high:

                    @pl.when(t == OFFSETS[m] + 1)
                    def _(m=m):
                        ring_start(m)

            for m in range(4):
                s = t - OFFSETS[m]
                if low - OFFSETS[m] > 8 or high - OFFSETS[m] < 1:
                    continue

                @pl.when((s >= 1) & (s <= 8))
                def _(m=m, s=s):
                    ring_tick(m, s)

            if work is not None:
                work(t)
            return 0

        lax.fori_loop(low, high + 1, body, 0)

    def gather_copy(layer, i):
        return remote(
            mine.at[layer], xs.at[layer, group], gather_send.at[layer, i], gather_recv.at[layer, group],
            at((x + i * (1 - c)) % 4, z, (y + i * c) % 4, yh),
        )

    def pass_y_copy(layer, i, j):
        g = ((x + i) % 4) * 4 + yl * 2
        return remote(
            xs.at[layer, g], xs.at[layer, g], pass_y_send.at[layer, i, j], gather_recv.at[layer, g], at(x, z, (y + j) % 4, c)
        )

    def pass_x_copy(layer, i, j):
        g = x * 4 + i * 2 + 1
        return remote(
            xs.at[layer, g], xs.at[layer, g], pass_x_send.at[layer, i, j], gather_recv.at[layer, g], at((x + j) % 4, z, y, c)
        )

    def arrive(layer, g):
        @pl.when((g != group) | (yh != c))
        def _():
            remote(xs.at[layer, g], xs.at[layer, g], gather_send.at[layer, 0], gather_recv.at[layer, g], sibling).wait_recv()

    def gather_start(layer):
        for i in range(1, 4):
            gather_copy(layer, i).start()

        @pl.when(c != yh)
        def _():
            gather_copy(layer, 0).start()

        @pl.when(c == yh)
        def _():
            xs[layer, group] = mine[layer]

    def gather_pass(layer):
        for i in range(4):

            @pl.when(c == yh)
            def _(i=i):
                arrive(layer, ((x + i) % 4) * 4 + yl * 2)
                for j in range(1, 4):
                    pass_y_copy(layer, i, j).start()

            if i < 2:
                arrive(layer, x * 4 + i * 2 + 1)
                for j in range(1, 4):
                    pass_x_copy(layer, i, j).start()

    def gather_wait(layer, g):
        passed_y = (yh == c) & (g % 2 == 0) & ((g // 2) % 2 == yl)
        passed_x = (g % 2 == 1) & (g // 4 == x)

        @pl.when(jnp.logical_not(passed_y | passed_x))
        def _():
            arrive(layer, g)

    def begin_up():
        acc[...] = jnp.zeros_like(acc)
        acc_rest[...] = jnp.zeros_like(acc_rest)
        squares[...] = jnp.zeros_like(squares)

    def up_unit(layer, zz):
        m = 2 * layer
        gather_wait(layer, zz)
        weights_wait(m, zz)
        main, rest = weight_tiles(weights[m, zz * 2], weights[m, zz * 2 + 1])
        rows = xs[layer, zz]
        acc[...] += dot(rows, main)
        acc_rest[...] += dot_nt(rows, rest)
        wide = rows.astype(jnp.float32)
        wide = wide * wide
        squares[...] += wide[:, :128] + wide[:, 128:]

    def end_up():
        scale = lax.rsqrt(jnp.sum(squares[...], axis=1, keepdims=True) * (1.0 / DV) + EPSILON)

        def act(v):
            v = v * scale
            return (0.5 * v * (1.0 + jnp.tanh(0.7978845608028654 * (v + 0.044715 * (v * v * v))))).astype(jnp.bfloat16)

        hid[...] = act(acc[...])
        hid_rest[...] = act(acc_rest[...])

    def one_copy(layer, g):
        gx, gy, gc = g // 4, (g // 2) % 2, g % 2
        return remote(
            staged.at[layer, g],
            first_sum.at[layer, (1 - gc) * (gx // 2) + gc * (2 + gy), (1 - gc) * y + gc * x],
            one_send.at[layer, g],
            one_recv.at[layer, (1 - gc) * (gx // 2) + gc * (2 + gy), (1 - gc) * y + gc * x],
            at((1 - gc) * x + gc * gx, z, (1 - gc) * (c * 2 + gy) + gc * y, (1 - gc) * (gx % 2) + gc * c),
        )

    def to_self(g):
        gx, gy, gc = g // 4, (g // 2) % 2, g % 2
        return ((gc == 0) & (c * 2 + gy == y) & (gx % 2 == c)) | ((gc == 1) & (gx == x))

    def down_unit(layer, zz):
        m = 2 * layer + 1
        weights_wait(m, zz)
        main, rest = weight_tiles(weights[m, zz * 2], weights[m, zz * 2 + 1])
        part = (dot_nt(hid[...], main) + dot(hid_rest[...], rest)).astype(jnp.bfloat16)

        gx, gy, gc = zz // 4, (zz // 2) % 2, zz % 2

        @pl.when(to_self(zz))
        def _():
            first_sum[layer, (1 - gc) * (gx // 2) + gc * (2 + gy), (1 - gc) * y + gc * x] = part

        @pl.when(jnp.logical_not(to_self(zz)))
        def _():
            staged[layer, zz] = part
            one_copy(layer, zz).start()

    def two_copy(layer, k):
        if k < 2:
            device, src = at(2 * k + c, z, y, 0), x
        else:
            device, src = at(x, z, c * 2 + k - 2, 1), y
        return remote(
            staged_sum.at[layer, k], second_sum.at[layer, src], two_send.at[layer, k], two_recv.at[layer, src], device
        )

    def two_self(k):
        return (2 * k + c == x) & (c == 0) if k < 2 else (y == c * 2 + k - 2) & (c == 1)

    def collect(layer):
        for k in (0, 2, 1, 3):
            total = None
            for src in range(4):

                @pl.when((src != y) | (yh != c) if k < 2 else src != x)
                def _(k=k, src=src):
                    remote(
                        staged.at[layer, 0], first_sum.at[layer, k, src], one_send.at[layer, 0], one_recv.at[layer, k, src], sibling
                    ).wait_recv()

                part = first_sum[layer, k, src].astype(jnp.float32)
                total = part if total is None else total + part
            total = total.astype(jnp.bfloat16)

            @pl.when(two_self(k))
            def _(k=k, total=total):
                second_sum[layer, x if k < 2 else y] = total

            @pl.when(jnp.logical_not(two_self(k)))
            def _(k=k, total=total):
                staged_sum[layer, k] = total
                two_copy(layer, k).start()

    def own_total(layer):
        total = mine[layer].astype(jnp.float32)
        for src in range(4):

            @pl.when(jnp.logical_not(((c == 0) & (src == x) & (x % 2 == 0)) | ((c == 1) & (src == y) & (yh == 1))))
            def _(src=src):
                remote(
                    staged_sum.at[layer, 0], second_sum.at[layer, src], two_send.at[layer, 0], two_recv.at[layer, src], sibling
                ).wait_recv()

            total = total + second_sum[layer, src].astype(jnp.float32)
        return total.astype(jnp.bfloat16)

    def groups(run):
        def body(i, _):
            run(((x + 1 + i // 4) % 4) * 4 + ((yl + i // 2) % 2) * 2 + i % 2)
            return 0

        lax.fori_loop(0, 16, body, 0)

    def units(run, low, high):
        def body(i, _):
            d = (i + 1) // 2
            run((z + jnp.where(i % 2 == 1, d, NZ - d)) % NZ)
            return 0

        lax.fori_loop(low, high, body, 0)

    for m in range(4):
        if OFFSETS[m] == 0:
            ring_start(m)
    gather_start(0)
    begin_up()
    r, q = iota((32 * CAP, 32 * SLOT), 0), iota((32 * CAP, 32 * SLOT), 1)
    squeeze[...] = one_hot(((q & 15) < CAP) & (r == (q >> 4) * CAP + (q & 15)))
    ticks(1, 2)
    gather_pass(0)
    ticks(3, 8)
    units(functools.partial(up_unit, 0), 0, 16)
    end_up()
    groups(functools.partial(down_unit, 0))
    begin_up()
    ticks(9, 10)
    collect(0)
    ticks(11, 11)
    mine[1] = own_total(0)
    gather_start(1)
    ticks(12, LAST)
    gather_pass(1)
    units(functools.partial(up_unit, 1), 0, 16)
    end_up()
    groups(functools.partial(down_unit, 1))
    collect(1)
    second = own_total(1)
    outbox[...] = dot(pick[...], second).astype(jnp.bfloat16).reshape(32, SLOT, LANES)

    def route_copy(d, s):
        return remote(outbox.at[d], inbox.at[s], route_send.at[d], route_recv.at[s], {"dp": d})

    def route_start(i, _):
        route_copy((dp + i) % 32, dp).start()
        return 0

    lax.fori_loop(1, 32, route_start, 0)
    inbox[dp] = outbox[dp]

    for m in range(4):
        for copy in start_copies(m):
            copy.wait_send()

    @pl.when(yh != c)
    def _():
        for m in range(4):
            lane_copy(m).wait_send()

    def drain_ring(i, _):
        m, s = i // 8, i % 8 + 1
        a, b = (z + NZ - s) % NZ, (z + s) % NZ
        for ch in range(CHUNKS):

            @pl.when((s < 7) | ((s == 7) & (ch == 0)))
            def _(ch=ch):
                up_copy(m, a, ch).wait_send()

            @pl.when((s < 7) | ((s == 7) & (ch == 1)))
            def _(ch=ch):
                down_copy(m, b, ch).wait_send()

        sib_copy(m, a, c).wait_send()

        @pl.when(s < 8)
        def _():
            sib_copy(m, b, c).wait_send()

        return 0

    lax.fori_loop(0, 32, drain_ring, 0)
    for layer in range(2):

        for i in range(1, 4):
            gather_copy(layer, i).wait_send()

        @pl.when(c != yh)
        def _(layer=layer):
            gather_copy(layer, 0).wait_send()

        @pl.when(c == yh)
        def _(layer=layer):
            for i in range(4):
                for j in range(1, 4):
                    pass_y_copy(layer, i, j).wait_send()

        for i in range(2):
            for j in range(1, 4):
                pass_x_copy(layer, i, j).wait_send()

        def drain_one(g, _, layer=layer):
            @pl.when(jnp.logical_not(to_self(g)))
            def _():
                one_copy(layer, g).wait_send()

            return 0

        lax.fori_loop(0, 16, drain_one, 0)

        for k in range(4):

            @pl.when(jnp.logical_not(two_self(k)))
            def _(layer=layer, k=k):
                two_copy(layer, k).wait_send()

    def route_wait(i, _):
        route_copy((dp + i) % 32, (dp + i) % 32).wait()
        return 0

    lax.fori_loop(1, 32, route_wait, 0)
    rows = dot(squeeze[...], inbox[...].reshape(32 * SLOT, LANES)).astype(jnp.bfloat16)
    f = iota((2 * HALF, LANES), 0)
    narrow = one_hot(iota((2 * HALF, LANES), 1) == f + jnp.where(f < HALF, 0, 28))
    out_ref[...] = dot_nt(narrow, rows).astype(jnp.bfloat16)


def on_device(patches, up_first, down_first, up_second, down_second, targets):
    bf16, dma = jnp.bfloat16, pltpu.SemaphoreType.DMA
    vmem, anywhere = pl.BlockSpec(memory_space=pltpu.VMEM), pl.BlockSpec(memory_space=pl.ANY)
    placed = pl.pallas_call(
        kernel,
        out_shape=jax.ShapeDtypeStruct((2 * HALF, 32 * CAP), bf16),
        in_specs=[anywhere] * 5 + [vmem],
        out_specs=vmem,
        scratch_shapes=[
            pltpu.VMEM((ROWS, 2 * HALF), bf16),
            pltpu.VMEM((4, 400, HALF), bf16),
            pltpu.VMEM((4, PACK, 128), bf16),
            dma((5,)),
            pltpu.VMEM((4, 32, PACK, 128), bf16),
            pltpu.VMEM((2, 16, ROWS, LANES), bf16),
            pltpu.VMEM((ROWS, 384), jnp.float32),
            pltpu.VMEM((ROWS, 16), jnp.float32),
            pltpu.VMEM((ROWS, 128), jnp.float32),
            pltpu.VMEM((ROWS, 384), bf16),
            pltpu.VMEM((ROWS, 16), bf16),
            pltpu.VMEM((2, 16, ROWS, LANES), bf16),
            pltpu.VMEM((2, 4, 4, ROWS, LANES), bf16),
            pltpu.VMEM((2, 4, ROWS, LANES), bf16),
            pltpu.VMEM((2, 4, ROWS, LANES), bf16),
            pltpu.VMEM((2, ROWS, LANES), bf16),
            pltpu.VMEM((32 * SLOT, ROWS), bf16),
            pltpu.VMEM((32 * CAP, 32 * SLOT), bf16),
            pltpu.VMEM((32, SLOT, LANES), bf16),
            pltpu.VMEM((32, SLOT, LANES), bf16),
            dma((4,)), dma((4,)),
            dma((4, NZ, CHUNKS)), dma((4, NZ, CHUNKS)), dma((4, NZ, CHUNKS)),
            dma((4, NZ)), dma((4, NZ)),
            dma((2, 4)), dma((2, 16)), dma((2, 4, 4)), dma((2, 2, 4)),
            dma((2, 16)), dma((2, 4, 4)),
            dma((2, 4)), dma((2, 4)),
            dma((32,)), dma((32,)),
        ],
        compiler_params=pltpu.CompilerParams(
            collective_id=0, has_side_effects=True, vmem_limit_bytes=60 * 1024 * 1024
        ),
    )(patches, up_first.T, down_first, up_second.T, down_second, targets.reshape(1, ROWS))
    return placed.T


def solution(mesh):
    in_specs = (
        P("dp", ("section", "mp")),
        P("dp", ("section", "mp")),
        P(("section", "mp"), "dp"),
        P("dp", ("section", "mp")),
        P(("section", "mp"), "dp"),
        P("dp", None),
    )
    return jax.shard_map(
        on_device, mesh=mesh, in_specs=in_specs, out_specs=P("dp", ("section", "mp")), check_vma=False
    )
```

```python
import functools

import jax
import jax.numpy as jnp
from jax import lax
from jax.experimental import pallas as pl
from jax.experimental.pallas import tpu as pltpu
from jax.sharding import PartitionSpec as P

MESH = pl.DeviceIdType.MESH
EPSILON = 1e-06
DV = 3200
ROWS = 192
NZ = 16
HALF = 100
PACK = 320
OFFSETS = (0, 0, 7, 7)
LAST = 15
CAP = 12
SLOT = 16


def remote(src, dst, send, recv, device):
    return pltpu.make_async_remote_copy(
        src_ref=src, dst_ref=dst, send_sem=send, recv_sem=recv, device_id=device, device_id_type=MESH
    )


def one_hot(mask):
    return jnp.where(mask, 1.0, 0.0).astype(jnp.bfloat16)


def iota(shape, axis):
    return lax.broadcasted_iota(jnp.int32, shape, axis)


def pack(block):
    turned = dot_nt(one_hot(iota((HALF, HALF), 0) == iota((HALF, HALF), 1)), block[0:384])
    tiles = [turned[:, 128 * j : 128 * j + 128] for j in range(3)]
    ends = jnp.concatenate([tile[96:100] for tile in tiles] + [jnp.zeros((4, 128), jnp.float32)], axis=0)
    return jnp.concatenate([tile[0:96].astype(jnp.bfloat16) for tile in tiles] + [ends.astype(jnp.bfloat16)], axis=0)


def weight_tiles(block):
    ends = block[288:304].astype(jnp.float32)
    none = jnp.zeros((12, 128), jnp.float32)
    ends = [jnp.concatenate([ends[4 * j : 4 * j + 4], none], axis=0).astype(jnp.bfloat16) for j in range(3)]
    rows = [jnp.concatenate([block[96 * j : 96 * j + 96] for j in range(3)], axis=1), jnp.concatenate(ends, axis=1)]
    return jnp.concatenate(rows + [jnp.zeros((16, 384), jnp.bfloat16)], axis=0), block[304:320]


def wrap(v, n):
    return jnp.where(v >= n, v - n, v)


def split(v):
    high = jnp.where(v >= 2, 1, 0)
    return high, v - 2 * high


def dot(a, b):
    return jnp.dot(a, b, preferred_element_type=jnp.float32)


def dot_nt(a, b):
    return lax.dot_general(a, b, (((1,), (1,)), ((), ())), preferred_element_type=jnp.float32)


def kernel(
    x_hbm, w0_hbm, w1_hbm, w2_hbm, w3_hbm, trow_ref, out_ref,
    x_ref, w_ref, packed, load_sem, weights, xs, acc, acc_rest, squares, hid, hid_rest, staged, first_sum, staged_sum, second_sum, mine,
    pick, squeeze, outbox, inbox,
    lane_send, lane_recv, ring_send, ring_recv, sib_send, sib_recv,
    gather_send, extra_send, pass_send, gather_recv, rest_recv, one_send, one_recv, two_send, two_recv, route_send, route_recv,
):
    x, dp, mp = lax.axis_index("section"), lax.axis_index("dp"), lax.axis_index("mp")
    z, yh, yl, c = dp // 2, dp % 2, mp // 2, mp % 2
    y = yh * 2 + yl
    group = x * 4 + mp

    def at(xx, zz, yy, cc):
        high, low = split(yy)
        return {"section": xx, "dp": zz * 2 + high, "mp": low * 2 + cc}

    above, below = wrap(z + 1, NZ), wrap(z + NZ - 1, NZ)
    up, down = at(x, above, y, c), at(x, below, y, c)
    sibling = at(x, z, y, 1 - c)
    lane_y, lane_c = c * 2 + yl, yh
    lane, lane_sibling = at(x, z, lane_y, lane_c), at(x, z, lane_y, 1 - lane_c)
    lane_up, lane_down = at(x, above, lane_y, lane_c), at(x, below, lane_y, lane_c)

    barrier = pltpu.get_barrier_semaphore()

    for i in range(1, 32):
        device = at(wrap(x + i // 8, 4), z, wrap(y + (i // 2) % 4, 4), wrap(c + i % 2, 2))
        pl.semaphore_signal(barrier, inc=1, device_id=device, device_id_type=MESH)
    for device in (up, down, lane_up, lane_down):
        pl.semaphore_signal(barrier, inc=1, device_id=device, device_id_type=MESH)

    loads = [pltpu.make_async_copy(x_hbm, x_ref, load_sem.at[4])]
    loads += [
        pltpu.make_async_copy(ref, w_ref.at[m], load_sem.at[m]) for m, ref in enumerate((w0_hbm, w1_hbm, w2_hbm, w3_hbm))
    ]
    for load in loads:
        load.start()

    def prepare(m):
        loads[1 + m].wait()
        packed[m, 0:304] = pack(w_ref[m])
        packed[m, 304:320] = jnp.zeros((16, 128), jnp.bfloat16)
        packed[m, 304:320, 0:HALF] = w_ref[m, 384:400]

    prepare(0)
    prepare(1)
    pl.semaphore_wait(barrier, 35)

    def landed(ref, sem):
        pltpu.make_async_copy(ref, ref, sem).wait()

    def slot(m, zz, cc):
        return weights.at[m, zz * 2 + cc]

    def up_copy(m, zz):
        return remote(slot(m, zz, c), slot(m, zz, c), ring_send, ring_recv.at[m, zz], up)

    def down_copy(m, zz):
        return remote(slot(m, zz, c), slot(m, zz, c), ring_send, ring_recv.at[m, zz], down)

    def sib_copy(m, zz):
        return remote(slot(m, zz, c), slot(m, zz, c), sib_send, sib_recv.at[m], sibling)

    def lane_copy(m):
        return remote(packed.at[m], slot(m, z, lane_c), lane_send, lane_recv.at[m], lane)

    def ring_start(m):
        for device in (lane_up, lane_down):
            remote(packed.at[m], slot(m, z, lane_c), ring_send, ring_recv.at[m, z], device).start()
        remote(packed.at[m], slot(m, z, lane_c), sib_send, sib_recv.at[m], lane_sibling).start()

        @pl.when(yh != c)
        def _():
            lane_copy(m).start()

        @pl.when(yh == c)
        def _():
            weights[m, z * 2 + c] = packed[m]

    def weights_wait(m):
        landed(weights.at[m, pl.ds(0, NZ)], sib_recv.at[m])

        @pl.when(yh != c)
        def _():
            landed(weights.at[m, 0], lane_recv.at[m])

    def ring_tick(m, s):
        a, b = wrap(z + NZ - s, NZ), wrap(z + s, NZ)
        up_copy(m, a).wait_recv()

        @pl.when((s < 7) | ((s == 7) & (m % 2 == 0)))
        def _():
            up_copy(m, a).start()

        @pl.when(s < 8)
        def _():
            down_copy(m, b).wait_recv()

        @pl.when((s < 7) | ((s == 7) & (m % 2 == 1)))
        def _():
            down_copy(m, b).start()

        sib_copy(m, a).start()

        @pl.when(s < 8)
        def _():
            sib_copy(m, b).start()

    def ticks(low, high, work=None):
        def body(t, _):
            for m in range(4):
                if OFFSETS[m] and low <= OFFSETS[m] + 1 <= high:

                    @pl.when(t == OFFSETS[m] + 1)
                    def _(m=m):
                        ring_start(m)

            for m in range(4):
                s = t - OFFSETS[m]
                if low - OFFSETS[m] > 8 or high - OFFSETS[m] < 1:
                    continue

                @pl.when((s >= 1) & (s <= 8))
                def _(m=m, s=s):
                    ring_tick(m, s)

            if work is not None:
                work(t)
            return 0

        lax.fori_loop(low, high + 1, body, 0)

    def gather_copy(part, i):
        return remote(
            mine.at[part], xs.at[part, group], gather_send if i else extra_send, gather_recv.at[part, (1 - c) * x + c * (4 + yl)],
            at(wrap(x + i * (1 - c), 4), z, wrap(y + i * c, 4), yh),
        )

    def pass_y_copy(part, i, j):
        g = wrap(x + i, 4) * 4 + yl * 2
        return remote(
            xs.at[part, g], xs.at[part, g], pass_send, rest_recv.at[part], at(x, z, wrap(y + j, 4), c)
        )

    def pass_x_copy(part, i, j):
        g = x * 4 + i * 2 + 1
        return remote(
            xs.at[part, g], xs.at[part, g], gather_send, rest_recv.at[part], at(wrap(x + j, 4), z, y, c)
        )

    def arrive(part, g, k):
        @pl.when((g != group) | (yh != c))
        def _():
            landed(xs.at[part, 0], gather_recv.at[part, k])

    def gather_start(part):
        for i in range(1, 4):
            gather_copy(part, i).start()

        @pl.when(c != yh)
        def _():
            gather_copy(part, 0).start()

        @pl.when(c == yh)
        def _():
            xs[part, group] = mine[part]

    def gather_pass(part):
        for i in range(4):

            @pl.when(c == yh)
            def _(i=i):
                arrive(part, wrap(x + i, 4) * 4 + yl * 2, wrap(x + i, 4))
                for j in range(1, 4):
                    pass_y_copy(part, i, j).start()

            if i < 2:
                arrive(part, x * 4 + i * 2 + 1, 4 + i)
                for j in range(1, 4):
                    pass_x_copy(part, i, j).start()

    def gather_rest(part):
        @pl.when(yh == c)
        def _():
            landed(xs.at[part, pl.ds(0, 10)], rest_recv.at[part])

        @pl.when(yh != c)
        def _():
            landed(xs.at[part, pl.ds(0, 14)], rest_recv.at[part])

    def begin_up():
        acc[...] = jnp.zeros_like(acc)
        acc_rest[...] = jnp.zeros_like(acc_rest)
        squares[...] = jnp.zeros_like(squares)

    def up_unit(layer, zz):
        m = 2 * layer
        first, second = weight_tiles(weights[m, zz * 2]), weight_tiles(weights[m, zz * 2 + 1])
        halves = xs[2 * layer, zz], xs[2 * layer + 1, zz]
        rows = jnp.concatenate(halves, axis=1)
        acc[...] += dot(rows, jnp.concatenate([first[0], second[0]], axis=0))
        acc_rest[...] += dot_nt(rows, jnp.concatenate([first[1], second[1]], axis=1))
        for half in halves:
            wide = half.astype(jnp.float32)
            squares[...] += wide * wide

    def end_up():
        scale = lax.rsqrt(jnp.sum(squares[...], axis=1, keepdims=True) * (1.0 / DV) + EPSILON)

        def act(v):
            v = v * scale
            return (0.5 * v * (1.0 + jnp.tanh(0.7978845608028654 * (v + 0.044715 * (v * v * v))))).astype(jnp.bfloat16)

        hid[...] = act(acc[...])
        hid_rest[...] = act(acc_rest[...])

    def one_place(gx, gy, gc):
        return (split(gx)[0], y) if gc == 0 else (2 + gy, x)

    def one_copy(part, gx, gy, gc):
        k, src = one_place(gx, gy, gc)
        return remote(
            staged.at[part, gx * 4 + gy * 2 + gc], first_sum.at[part, k, src], one_send, one_recv.at[part, k],
            at(x, z, c * 2 + gy, split(gx)[1]) if gc == 0 else at(gx, z, y, c),
        )

    def to_self(gx, gy, gc):
        return (c * 2 + gy == y) & (split(gx)[1] == c) if gc == 0 else gx == x

    def down_unit(part, gx, gy, gc):
        m, half = 2 * (part // 2) + 1, part % 2

        main, rest = weight_tiles(weights[m, (gx * 4 + gy * 2 + gc) * 2 + half])
        total = (dot_nt(hid[...], main) + dot(hid_rest[...], rest)).astype(jnp.bfloat16)

        @pl.when(to_self(gx, gy, gc))
        def _():
            k, src = one_place(gx, gy, gc)
            first_sum[part, k, src] = total

        @pl.when(jnp.logical_not(to_self(gx, gy, gc)))
        def _():
            staged[part, gx * 4 + gy * 2 + gc] = total
            one_copy(part, gx, gy, gc).start()

    def two_copy(part, k):
        if k < 2:
            device, src = at(2 * k + c, z, y, 0), x
        else:
            device, src = at(x, z, c * 2 + k - 2, 1), y
        return remote(
            staged_sum.at[part, k], second_sum.at[part, src], two_send, two_recv.at[part], device
        )

    def two_self(k):
        return (2 * k + c == x) & (c == 0) if k < 2 else (y == c * 2 + k - 2) & (c == 1)

    def collect(part):
        for k in (0, 2, 1, 3):
            if k < 2:

                @pl.when(yh == c)
                def _(k=k):
                    landed(first_sum.at[part, k, pl.ds(0, 3)], one_recv.at[part, k])

                @pl.when(yh != c)
                def _(k=k):
                    landed(first_sum.at[part, k], one_recv.at[part, k])
            else:
                landed(first_sum.at[part, k, pl.ds(0, 3)], one_recv.at[part, k])
            total = None
            for src in range(4):
                term = first_sum[part, k, src].astype(jnp.float32)
                total = term if total is None else total + term
            total = total.astype(jnp.bfloat16)

            @pl.when(two_self(k))
            def _(k=k, total=total):
                second_sum[part, x if k < 2 else y] = total

            @pl.when(jnp.logical_not(two_self(k)))
            def _(k=k, total=total):
                staged_sum[part, k] = total
                two_copy(part, k).start()

    def own_total(part):
        with_self = ((c == 0) & (split(x)[1] == 0)) | ((c == 1) & (yh == 1))

        @pl.when(with_self)
        def _():
            landed(second_sum.at[part, pl.ds(0, 3)], two_recv.at[part])

        @pl.when(jnp.logical_not(with_self))
        def _():
            landed(second_sum.at[part], two_recv.at[part])

        total = mine[part].astype(jnp.float32)
        for src in range(4):
            total = total + second_sum[part, src].astype(jnp.float32)
        return total.astype(jnp.bfloat16)

    def groups(run):
        def body(i, _):
            gx = wrap(x + i, 4)
            for j in range(4):
                run(gx, wrap(yl + j // 2, 2), j % 2)
            return 0

        lax.fori_loop(1, 5, body, 0)

    def units(run):
        def body(s, _):
            run(wrap(z + s, NZ))
            run(wrap(z + NZ - s, NZ))
            return 0

        run(z)
        lax.fori_loop(1, 8, body, 0)
        run(wrap(z + 8, NZ))

    def route_copy(half, d, s):
        return remote(
            outbox.at[half, d], inbox.at[half, s], route_send, route_recv.at[half], {"dp": d}
        )

    def route_start(half):
        outbox[half] = dot(pick[...], own_total(2 + half)).astype(jnp.bfloat16).reshape(32, SLOT, 128)

        def body(i, _):
            for far in (16 - i, 16 + i):
                d = wrap(dp + far, 32)
                route_copy(half, d, dp).start()
            return 0

        route_copy(half, wrap(dp + 16, 32), dp).start()
        lax.fori_loop(1, 16, body, 0)
        inbox[half, dp] = outbox[half, dp]

    ring_start(0)
    ring_start(1)
    loads[0].wait()
    rows = x_ref[...]
    for half in range(2):
        shape = (2 * HALF, 128)
        widen = one_hot((iota(shape, 0) == iota(shape, 1) + half * HALF) & (iota(shape, 1) < HALF))
        mine[half] = dot(rows, widen).astype(jnp.bfloat16)
        gather_start(half)
    prepare(2)
    prepare(3)
    begin_up()
    trow = trow_ref[...]
    named = jnp.where(iota((32, ROWS), 0) == trow, 1.0, 0.0)
    before = one_hot(iota((ROWS, ROWS), 0) < iota((ROWS, ROWS), 1))
    position = jnp.sum(named * dot(named.astype(jnp.bfloat16), before), axis=0, keepdims=True).astype(jnp.int32)
    pick[...] = one_hot(iota((32 * SLOT, ROWS), 0) == trow * SLOT + position)

    r, q = iota((32 * CAP, 32 * SLOT), 0), iota((32 * CAP, 32 * SLOT), 1)
    squeeze[...] = one_hot(((q & 15) < CAP) & (r == (q >> 4) * CAP + (q & 15)))
    ticks(1, 2)
    gather_pass(0)
    gather_pass(1)
    ticks(3, 8)
    gather_rest(0)
    gather_rest(1)
    weights_wait(0)
    units(functools.partial(up_unit, 0))
    end_up()
    weights_wait(1)
    groups(functools.partial(down_unit, 0))
    groups(functools.partial(down_unit, 1))
    begin_up()
    ticks(9, 10)
    collect(0)
    collect(1)
    ticks(11, 11)
    mine[2] = own_total(0)
    gather_start(2)
    mine[3] = own_total(1)
    gather_start(3)
    ticks(12, 12)
    gather_pass(2)
    gather_pass(3)
    ticks(13, LAST)
    gather_rest(2)
    gather_rest(3)
    weights_wait(2)
    units(functools.partial(up_unit, 1))
    end_up()
    weights_wait(3)
    groups(functools.partial(down_unit, 2))
    groups(functools.partial(down_unit, 3))
    collect(2)
    collect(3)
    route_start(0)
    route_start(1)

    for half in range(2):
        landed(inbox.at[half, pl.ds(0, 31)], route_recv.at[half])

    landed(weights.at[:, pl.ds(0, 15)], ring_send)
    landed(weights.at[:, pl.ds(0, 16)], sib_send)
    landed(xs.at[:, pl.ds(0, 9)], gather_send)

    @pl.when(yh != c)
    def _():
        landed(weights.at[0, pl.ds(0, 4)], lane_send)
        landed(xs.at[:, 0], extra_send)
        landed(xs.at[:, pl.ds(0, 14)], one_send)

    @pl.when(yh == c)
    def _():
        landed(xs.at[:, pl.ds(0, 12)], pass_send)
        landed(xs.at[:, pl.ds(0, 12)], one_send)

    two_at_home = ((c == 0) & (split(x)[1] == 0)) | ((c == 1) & (yh == 1))

    @pl.when(two_at_home)
    def _():
        landed(staged_sum.at[:, pl.ds(0, 3)], two_send)

    @pl.when(jnp.logical_not(two_at_home))
    def _():
        landed(staged_sum, two_send)

    landed(inbox.at[:, pl.ds(0, 31)], route_send)
    total = None
    for half in range(2):
        rows = dot(squeeze[...], inbox[half].reshape(32 * SLOT, 128)).astype(jnp.bfloat16)
        shape = (2 * HALF, 128)
        narrow = one_hot((iota(shape, 0) == iota(shape, 1) + half * HALF) & (iota(shape, 1) < HALF))
        term = dot_nt(narrow, rows)
        total = term if total is None else total + term
    out_ref[...] = total.astype(jnp.bfloat16)


def on_device(patches, up_first, down_first, up_second, down_second, targets):
    bf16, dma = jnp.bfloat16, pltpu.SemaphoreType.DMA
    vmem, anywhere = pl.BlockSpec(memory_space=pltpu.VMEM), pl.BlockSpec(memory_space=pl.ANY)
    placed = pl.pallas_call(
        kernel,
        out_shape=jax.ShapeDtypeStruct((2 * HALF, 32 * CAP), bf16),
        in_specs=[anywhere] * 5 + [vmem],
        out_specs=vmem,
        scratch_shapes=[
            pltpu.VMEM((ROWS, 2 * HALF), bf16),
            pltpu.VMEM((4, 400, HALF), bf16),
            pltpu.VMEM((4, PACK, 128), bf16),
            dma((5,)),
            pltpu.VMEM((4, 32, PACK, 128), bf16),
            pltpu.VMEM((4, 16, ROWS, 128), bf16),
            pltpu.VMEM((ROWS, 384), jnp.float32),
            pltpu.VMEM((ROWS, 16), jnp.float32),
            pltpu.VMEM((ROWS, 128), jnp.float32),
            pltpu.VMEM((ROWS, 384), bf16),
            pltpu.VMEM((ROWS, 16), bf16),
            pltpu.VMEM((4, 16, ROWS, 128), bf16),
            pltpu.VMEM((4, 4, 4, ROWS, 128), bf16),
            pltpu.VMEM((4, 4, ROWS, 128), bf16),
            pltpu.VMEM((4, 4, ROWS, 128), bf16),
            pltpu.VMEM((4, ROWS, 128), bf16),
            pltpu.VMEM((32 * SLOT, ROWS), bf16),
            pltpu.VMEM((32 * CAP, 32 * SLOT), bf16),
            pltpu.VMEM((2, 32, SLOT, 128), bf16),
            pltpu.VMEM((2, 32, SLOT, 128), bf16),
            dma(()), dma((4,)),
            dma(()), dma((4, NZ)),
            dma(()), dma((4,)),
            dma(()), dma(()), dma(()), dma((4, 6)), dma((4,)),
            dma(()), dma((4, 4)),
            dma(()), dma((4,)),
            dma(()), dma((2,)),
        ],
        compiler_params=pltpu.CompilerParams(
            collective_id=0, has_side_effects=True, vmem_limit_bytes=60 * 1024 * 1024
        ),
    )(patches, up_first.T, down_first, up_second.T, down_second, targets.reshape(1, ROWS))
    return placed.T


def solution(mesh):
    in_specs = (
        P("dp", ("section", "mp")),
        P("dp", ("section", "mp")),
        P(("section", "mp"), "dp"),
        P("dp", ("section", "mp")),
        P(("section", "mp"), "dp"),
        P("dp", None),
    )
    return jax.shard_map(
        on_device, mesh=mesh, in_specs=in_specs, out_specs=P("dp", ("section", "mp")), check_vma=False
    )
```

```python
import functools

import jax
import jax.numpy as jnp
from jax import lax
from jax.experimental import pallas as pl
from jax.experimental.pallas import tpu as pltpu
from jax.sharding import PartitionSpec as P

MESH = pl.DeviceIdType.MESH
EPSILON = 1e-06
DV = 3200
ROWS = 192
NZ = 16
HALF = 100
PACK = 320
CHUNKS = 2
CHUNK = PACK // CHUNKS
OFFSETS = (0, 0, 7, 7)
LAST = 15
CAP = 12
SLOT = 16


def remote(src, dst, send, recv, device):
    return pltpu.make_async_remote_copy(
        src_ref=src, dst_ref=dst, send_sem=send, recv_sem=recv, device_id=device, device_id_type=MESH
    )


def one_hot(mask):
    return jnp.where(mask, 1.0, 0.0).astype(jnp.bfloat16)


def iota(shape, axis):
    return lax.broadcasted_iota(jnp.int32, shape, axis)


def pack(block):
    turned = dot_nt(one_hot(iota((HALF, HALF), 0) == iota((HALF, HALF), 1)), block[0:384])
    tiles = [turned[:, 128 * j : 128 * j + 128] for j in range(3)]
    ends = jnp.concatenate([tile[96:100] for tile in tiles] + [jnp.zeros((4, 128), jnp.float32)], axis=0)
    return jnp.concatenate([tile[0:96].astype(jnp.bfloat16) for tile in tiles] + [ends.astype(jnp.bfloat16)], axis=0)


def weight_tiles(block):
    ends = block[288:304].astype(jnp.float32)
    none = jnp.zeros((12, 128), jnp.float32)
    ends = [jnp.concatenate([ends[4 * j : 4 * j + 4], none], axis=0).astype(jnp.bfloat16) for j in range(3)]
    rows = [jnp.concatenate([block[96 * j : 96 * j + 96] for j in range(3)], axis=1), jnp.concatenate(ends, axis=1)]
    return jnp.concatenate(rows + [jnp.zeros((16, 384), jnp.bfloat16)], axis=0), block[304:320]


def wrap(v, n):
    return jnp.where(v >= n, v - n, v)


def split(v):
    high = jnp.where(v >= 2, 1, 0)
    return high, v - 2 * high


def dot(a, b):
    return jnp.dot(a, b, preferred_element_type=jnp.float32)


def dot_nt(a, b):
    return lax.dot_general(a, b, (((1,), (1,)), ((), ())), preferred_element_type=jnp.float32)


def kernel(
    x_hbm, w0_hbm, w1_hbm, w2_hbm, w3_hbm, trow_ref, out_ref,
    x_ref, w_ref, packed, load_sem, weights, xs, acc, acc_rest, squares, hid, hid_rest, staged, first_sum, staged_sum, second_sum, mine,
    pick, squeeze, outbox, inbox,
    lane_send, lane_recv, ring_send, ring_recv, sib_send, sib_recv,
    gather_send, extra_send, pass_send, gather_recv, rest_recv, one_send, one_recv, two_send, two_recv, route_send, route_recv,
):
    x, dp, mp = lax.axis_index("section"), lax.axis_index("dp"), lax.axis_index("mp")
    z, yh, yl, c = dp // 2, dp % 2, mp // 2, mp % 2
    y = yh * 2 + yl
    group = x * 4 + mp

    def at(xx, zz, yy, cc):
        high, low = split(yy)
        return {"section": xx, "dp": zz * 2 + high, "mp": low * 2 + cc}

    above, below = wrap(z + 1, NZ), wrap(z + NZ - 1, NZ)
    up, down = at(x, above, y, c), at(x, below, y, c)
    sibling = at(x, z, y, 1 - c)
    lane_y, lane_c = c * 2 + yl, yh
    lane, lane_sibling = at(x, z, lane_y, lane_c), at(x, z, lane_y, 1 - lane_c)
    lane_up, lane_down = at(x, above, lane_y, lane_c), at(x, below, lane_y, lane_c)

    barrier = pltpu.get_barrier_semaphore()

    for i in range(1, 32):
        device = at(wrap(x + i // 8, 4), z, wrap(y + (i // 2) % 4, 4), wrap(c + i % 2, 2))
        pl.semaphore_signal(barrier, inc=1, device_id=device, device_id_type=MESH)
    for device in (up, down, lane_up, lane_down):
        pl.semaphore_signal(barrier, inc=1, device_id=device, device_id_type=MESH)

    loads = [pltpu.make_async_copy(x_hbm, x_ref, load_sem.at[4])]
    loads += [
        pltpu.make_async_copy(ref, w_ref.at[m], load_sem.at[m]) for m, ref in enumerate((w0_hbm, w1_hbm, w2_hbm, w3_hbm))
    ]
    for load in loads:
        load.start()

    def prepare(m):
        loads[1 + m].wait()
        packed[m, 0:304] = pack(w_ref[m])
        packed[m, 304:320] = jnp.zeros((16, 128), jnp.bfloat16)
        packed[m, 304:320, 0:HALF] = w_ref[m, 384:400]

    prepare(0)
    prepare(1)
    pl.semaphore_wait(barrier, 35)

    def landed(ref, sem):
        pltpu.make_async_copy(ref, ref, sem).wait()

    def slot(m, zz, cc):
        return weights.at[m, zz * 2 + cc]

    def piece(m, zz, cc, ch):
        return weights.at[m, zz * 2 + cc, pl.ds(ch * CHUNK, CHUNK)]

    def up_copy(m, zz, ch):
        return remote(piece(m, zz, c, ch), piece(m, zz, c, ch), ring_send, ring_recv.at[m, zz, ch], up)

    def down_copy(m, zz, ch):
        return remote(piece(m, zz, c, ch), piece(m, zz, c, ch), ring_send, ring_recv.at[m, zz, ch], down)

    def sib_copy(m, zz):
        return remote(slot(m, zz, c), slot(m, zz, c), sib_send, sib_recv.at[m], sibling)

    def lane_copy(m):
        return remote(packed.at[m], slot(m, z, lane_c), lane_send, lane_recv.at[m], lane)

    def ring_start(m):
        for ch in range(CHUNKS):
            src = packed.at[m, pl.ds(ch * CHUNK, CHUNK)]
            for device in (lane_up, lane_down):
                remote(src, piece(m, z, lane_c, ch), ring_send, ring_recv.at[m, z, ch], device).start()
        remote(packed.at[m], slot(m, z, lane_c), sib_send, sib_recv.at[m], lane_sibling).start()

        @pl.when(yh != c)
        def _():
            lane_copy(m).start()

        @pl.when(yh == c)
        def _():
            weights[m, z * 2 + c] = packed[m]

    def weights_wait(m):
        landed(weights.at[m, pl.ds(0, NZ)], sib_recv.at[m])

        @pl.when(yh != c)
        def _():
            landed(weights.at[m, 0], lane_recv.at[m])

    def ring_tick(m, s):
        a, b = wrap(z + NZ - s, NZ), wrap(z + s, NZ)
        for ch in range(CHUNKS):
            up_copy(m, a, ch).wait_recv()

            @pl.when((s < 7) | ((s == 7) & (m % 2 == 0)))
            def _(ch=ch):
                up_copy(m, a, ch).start()

            @pl.when(s < 8)
            def _(ch=ch):
                down_copy(m, b, ch).wait_recv()

            @pl.when((s < 7) | ((s == 7) & (m % 2 == 1)))
            def _(ch=ch):
                down_copy(m, b, ch).start()

        sib_copy(m, a).start()

        @pl.when(s < 8)
        def _():
            sib_copy(m, b).start()

    def ticks(low, high, which=range(4)):
        def body(t, _):
            for m in which:
                if OFFSETS[m] and low <= OFFSETS[m] + 1 <= high:

                    @pl.when(t == OFFSETS[m] + 1)
                    def _(m=m):
                        ring_start(m)

            for m in which:
                s = t - OFFSETS[m]
                if low - OFFSETS[m] > 8 or high - OFFSETS[m] < 1:
                    continue

                @pl.when((s >= 1) & (s <= 8))
                def _(m=m, s=s):
                    ring_tick(m, s)

            return 0

        lax.fori_loop(low, high + 1, body, 0)

    def gather_copy(part, i):
        return remote(
            mine.at[part], xs.at[part, group], gather_send if i else extra_send, gather_recv.at[part, (1 - c) * x + c * (4 + yl)],
            at(wrap(x + i * (1 - c), 4), z, wrap(y + i * c, 4), yh),
        )

    def pass_y_copy(part, i, j):
        g = wrap(x + i, 4) * 4 + yl * 2
        return remote(
            xs.at[part, g], xs.at[part, g], pass_send, rest_recv.at[part], at(x, z, wrap(y + j, 4), c)
        )

    def pass_x_copy(part, i, j):
        g = x * 4 + i * 2 + 1
        return remote(
            xs.at[part, g], xs.at[part, g], gather_send, rest_recv.at[part], at(wrap(x + j, 4), z, y, c)
        )

    def arrive(part, g, k):
        @pl.when((g != group) | (yh != c))
        def _():
            landed(xs.at[part, 0], gather_recv.at[part, k])

    def gather_start(part):
        for i in range(1, 4):
            gather_copy(part, i).start()

        @pl.when(c != yh)
        def _():
            gather_copy(part, 0).start()

        @pl.when(c == yh)
        def _():
            xs[part, group] = mine[part]

    def gather_pass(part):
        for i in range(4):

            @pl.when(c == yh)
            def _(i=i):
                arrive(part, wrap(x + i, 4) * 4 + yl * 2, wrap(x + i, 4))
                for j in range(1, 4):
                    pass_y_copy(part, i, j).start()

            if i < 2:
                arrive(part, x * 4 + i * 2 + 1, 4 + i)
                for j in range(1, 4):
                    pass_x_copy(part, i, j).start()

    def gather_rest(part):
        @pl.when(yh == c)
        def _():
            landed(xs.at[part, pl.ds(0, 10)], rest_recv.at[part])

        @pl.when(yh != c)
        def _():
            landed(xs.at[part, pl.ds(0, 14)], rest_recv.at[part])

    def begin_up():
        acc[...] = jnp.zeros_like(acc)
        acc_rest[...] = jnp.zeros_like(acc_rest)
        squares[...] = jnp.zeros_like(squares)

    def up_unit(layer, zz):
        m = 2 * layer
        first, second = weight_tiles(weights[m, zz * 2]), weight_tiles(weights[m, zz * 2 + 1])
        halves = xs[2 * layer, zz], xs[2 * layer + 1, zz]
        rows = jnp.concatenate(halves, axis=1)
        acc[...] += dot(rows, jnp.concatenate([first[0], second[0]], axis=0))
        acc_rest[...] += dot_nt(rows, jnp.concatenate([first[1], second[1]], axis=1))
        for half in halves:
            wide = half.astype(jnp.float32)
            squares[...] += wide * wide

    def end_up():
        scale = lax.rsqrt(jnp.sum(squares[...], axis=1, keepdims=True) * (1.0 / DV) + EPSILON)

        def act(v):
            v = v * scale
            return (0.5 * v * (1.0 + jnp.tanh(0.7978845608028654 * (v + 0.044715 * (v * v * v))))).astype(jnp.bfloat16)

        hid[...] = act(acc[...])
        hid_rest[...] = act(acc_rest[...])

    def one_place(gx, gy, gc):
        return (split(gx)[0], y) if gc == 0 else (2 + gy, x)

    def one_copy(part, gx, gy, gc):
        k, src = one_place(gx, gy, gc)
        return remote(
            staged.at[part, gx * 4 + gy * 2 + gc], first_sum.at[part, k, src], one_send, one_recv.at[part, k],
            at(x, z, c * 2 + gy, split(gx)[1]) if gc == 0 else at(gx, z, y, c),
        )

    def to_self(gx, gy, gc):
        return (c * 2 + gy == y) & (split(gx)[1] == c) if gc == 0 else gx == x

    def down_unit(part, gx, gy, gc):
        m, half = 2 * (part // 2) + 1, part % 2

        main, rest = weight_tiles(weights[m, (gx * 4 + gy * 2 + gc) * 2 + half])
        total = (dot_nt(hid[...], main) + dot(hid_rest[...], rest)).astype(jnp.bfloat16)

        @pl.when(to_self(gx, gy, gc))
        def _():
            k, src = one_place(gx, gy, gc)
            first_sum[part, k, src] = total

        @pl.when(jnp.logical_not(to_self(gx, gy, gc)))
        def _():
            staged[part, gx * 4 + gy * 2 + gc] = total
            one_copy(part, gx, gy, gc).start()

    def two_copy(part, k):
        if k < 2:
            device, src = at(2 * k + c, z, y, 0), x
        else:
            device, src = at(x, z, c * 2 + k - 2, 1), y
        return remote(
            staged_sum.at[part, k], second_sum.at[part, src], two_send, two_recv.at[part], device
        )

    def two_self(k):
        return (2 * k + c == x) & (c == 0) if k < 2 else (y == c * 2 + k - 2) & (c == 1)

    def collect(part):
        for k in (0, 2, 1, 3):
            if k < 2:

                @pl.when(yh == c)
                def _(k=k):
                    landed(first_sum.at[part, k, pl.ds(0, 3)], one_recv.at[part, k])

                @pl.when(yh != c)
                def _(k=k):
                    landed(first_sum.at[part, k], one_recv.at[part, k])
            else:
                landed(first_sum.at[part, k, pl.ds(0, 3)], one_recv.at[part, k])
            total = None
            for src in range(4):
                term = first_sum[part, k, src].astype(jnp.float32)
                total = term if total is None else total + term
            total = total.astype(jnp.bfloat16)

            @pl.when(two_self(k))
            def _(k=k, total=total):
                second_sum[part, x if k < 2 else y] = total

            @pl.when(jnp.logical_not(two_self(k)))
            def _(k=k, total=total):
                staged_sum[part, k] = total
                two_copy(part, k).start()

    def own_total(part):
        with_self = ((c == 0) & (split(x)[1] == 0)) | ((c == 1) & (yh == 1))

        @pl.when(with_self)
        def _():
            landed(second_sum.at[part, pl.ds(0, 3)], two_recv.at[part])

        @pl.when(jnp.logical_not(with_self))
        def _():
            landed(second_sum.at[part], two_recv.at[part])

        total = mine[part].astype(jnp.float32)
        for src in range(4):
            total = total + second_sum[part, src].astype(jnp.float32)
        return total.astype(jnp.bfloat16)

    def groups(run):
        def body(i, _):
            gx = wrap(x + i, 4)
            for j in range(4):
                run(gx, wrap(yl + j // 2, 2), j % 2)
            return 0

        lax.fori_loop(1, 5, body, 0)

    def units(run):
        def body(s, _):
            run(wrap(z + s, NZ))
            run(wrap(z + NZ - s, NZ))
            return 0

        run(z)
        lax.fori_loop(1, 8, body, 0)
        run(wrap(z + 8, NZ))

    def route_copy(half, d, s):
        return remote(
            outbox.at[half, d], inbox.at[half, s], route_send, route_recv.at[half], {"dp": d}
        )

    def route_start(half):
        outbox[half] = dot(pick[...], own_total(2 + half)).astype(jnp.bfloat16).reshape(32, SLOT, 128)

        def body(i, _):
            for far in (16 - i, 16 + i):
                d = wrap(dp + far, 32)
                route_copy(half, d, dp).start()
            return 0

        route_copy(half, wrap(dp + 16, 32), dp).start()
        lax.fori_loop(1, 16, body, 0)
        inbox[half, dp] = outbox[half, dp]

    ring_start(0)
    ring_start(1)
    loads[0].wait()
    rows = x_ref[...]
    for half in range(2):
        shape = (2 * HALF, 128)
        widen = one_hot((iota(shape, 0) == iota(shape, 1) + half * HALF) & (iota(shape, 1) < HALF))
        mine[half] = dot(rows, widen).astype(jnp.bfloat16)
        gather_start(half)
    prepare(2)
    prepare(3)
    begin_up()
    trow = trow_ref[...]
    named = jnp.where(iota((32, ROWS), 0) == trow, 1.0, 0.0)
    before = one_hot(iota((ROWS, ROWS), 0) < iota((ROWS, ROWS), 1))
    position = jnp.sum(named * dot(named.astype(jnp.bfloat16), before), axis=0, keepdims=True).astype(jnp.int32)
    pick[...] = one_hot(iota((32 * SLOT, ROWS), 0) == trow * SLOT + position)

    r, q = iota((32 * CAP, 32 * SLOT), 0), iota((32 * CAP, 32 * SLOT), 1)
    squeeze[...] = one_hot(((q & 15) < CAP) & (r == (q >> 4) * CAP + (q & 15)))
    ticks(1, 2)
    gather_pass(0)
    gather_pass(1)
    ticks(3, 8)
    gather_rest(0)
    gather_rest(1)
    weights_wait(0)
    units(functools.partial(up_unit, 0))
    end_up()
    weights_wait(1)
    groups(functools.partial(down_unit, 0))
    groups(functools.partial(down_unit, 1))
    begin_up()
    ticks(9, 10)
    collect(0)
    collect(1)
    ticks(11, 11)
    mine[2] = own_total(0)
    gather_start(2)
    mine[3] = own_total(1)
    gather_start(3)
    ticks(12, 12)
    gather_pass(2)
    gather_pass(3)
    ticks(13, LAST)
    gather_rest(2)
    gather_rest(3)
    weights_wait(2)
    units(functools.partial(up_unit, 1))
    end_up()
    weights_wait(3)
    groups(functools.partial(down_unit, 2))
    groups(functools.partial(down_unit, 3))
    collect(2)
    collect(3)
    route_start(0)
    route_start(1)

    landed(weights.at[:, pl.ds(0, 15)], ring_send)
    landed(weights.at[:, pl.ds(0, 16)], sib_send)
    landed(xs.at[:, pl.ds(0, 9)], gather_send)

    @pl.when(yh != c)
    def _():
        landed(weights.at[0, pl.ds(0, 4)], lane_send)
        landed(xs.at[:, 0], extra_send)
        landed(xs.at[:, pl.ds(0, 14)], one_send)

    @pl.when(yh == c)
    def _():
        landed(xs.at[:, pl.ds(0, 12)], pass_send)
        landed(xs.at[:, pl.ds(0, 12)], one_send)

    two_at_home = ((c == 0) & (split(x)[1] == 0)) | ((c == 1) & (yh == 1))

    @pl.when(two_at_home)
    def _():
        landed(staged_sum.at[:, pl.ds(0, 3)], two_send)

    @pl.when(jnp.logical_not(two_at_home))
    def _():
        landed(staged_sum, two_send)

    total = None
    for half in range(2):
        landed(inbox.at[half, pl.ds(0, 31)], route_recv.at[half])
        rows = dot(squeeze[...], inbox[half].reshape(32 * SLOT, 128)).astype(jnp.bfloat16)
        shape = (2 * HALF, 128)
        narrow = one_hot((iota(shape, 0) == iota(shape, 1) + half * HALF) & (iota(shape, 1) < HALF))
        term = dot_nt(narrow, rows)
        total = term if total is None else total + term
    out_ref[...] = total.astype(jnp.bfloat16)
    landed(inbox.at[:, pl.ds(0, 31)], route_send)


def on_device(patches, up_first, down_first, up_second, down_second, targets):
    bf16, dma = jnp.bfloat16, pltpu.SemaphoreType.DMA
    vmem, anywhere = pl.BlockSpec(memory_space=pltpu.VMEM), pl.BlockSpec(memory_space=pl.ANY)
    placed = pl.pallas_call(
        kernel,
        out_shape=jax.ShapeDtypeStruct((2 * HALF, 32 * CAP), bf16),
        in_specs=[anywhere] * 5 + [vmem],
        out_specs=vmem,
        scratch_shapes=[
            pltpu.VMEM((ROWS, 2 * HALF), bf16),
            pltpu.VMEM((4, 400, HALF), bf16),
            pltpu.VMEM((4, PACK, 128), bf16),
            dma((5,)),
            pltpu.VMEM((4, 32, PACK, 128), bf16),
            pltpu.VMEM((4, 16, ROWS, 128), bf16),
            pltpu.VMEM((ROWS, 384), jnp.float32),
            pltpu.VMEM((ROWS, 16), jnp.float32),
            pltpu.VMEM((ROWS, 128), jnp.float32),
            pltpu.VMEM((ROWS, 384), bf16),
            pltpu.VMEM((ROWS, 16), bf16),
            pltpu.VMEM((4, 16, ROWS, 128), bf16),
            pltpu.VMEM((4, 4, 4, ROWS, 128), bf16),
            pltpu.VMEM((4, 4, ROWS, 128), bf16),
            pltpu.VMEM((4, 4, ROWS, 128), bf16),
            pltpu.VMEM((4, ROWS, 128), bf16),
            pltpu.VMEM((32 * SLOT, ROWS), bf16),
            pltpu.VMEM((32 * CAP, 32 * SLOT), bf16),
            pltpu.VMEM((2, 32, SLOT, 128), bf16),
            pltpu.VMEM((2, 32, SLOT, 128), bf16),
            dma(()), dma((4,)),
            dma(()), dma((4, NZ, CHUNKS)),
            dma(()), dma((4,)),
            dma(()), dma(()), dma(()), dma((4, 6)), dma((4,)),
            dma(()), dma((4, 4)),
            dma(()), dma((4,)),
            dma(()), dma((2,)),
        ],
        compiler_params=pltpu.CompilerParams(
            collective_id=0, has_side_effects=True, vmem_limit_bytes=60 * 1024 * 1024
        ),
    )(patches, up_first.T, down_first, up_second.T, down_second, targets.reshape(1, ROWS))
    return placed.T


def solution(mesh):
    in_specs = (
        P("dp", ("section", "mp")),
        P("dp", ("section", "mp")),
        P(("section", "mp"), "dp"),
        P("dp", ("section", "mp")),
        P(("section", "mp"), "dp"),
        P("dp", None),
    )
    return jax.shard_map(
        on_device, mesh=mesh, in_specs=in_specs, out_specs=P("dp", ("section", "mp")), check_vma=False
    )
```

```python
import functools

import jax
import jax.numpy as jnp
from jax import lax
from jax.experimental import pallas as pl
from jax.experimental.pallas import tpu as pltpu
from jax.sharding import PartitionSpec as P

MESH = pl.DeviceIdType.MESH
EPSILON = 1e-06
DV = 3200
ROWS = 192
NZ = 16
HALF = 100
PACK = 320
CHUNKS = 2
CHUNK = PACK // CHUNKS
OFFSETS = (0, 0, 7, 7)
LAST = 15
CAP = 12
SLOT = 16


def remote(src, dst, send, recv, device):
    return pltpu.make_async_remote_copy(
        src_ref=src, dst_ref=dst, send_sem=send, recv_sem=recv, device_id=device, device_id_type=MESH
    )


def one_hot(mask):
    return jnp.where(mask, 1.0, 0.0).astype(jnp.bfloat16)


def iota(shape, axis):
    return lax.broadcasted_iota(jnp.int32, shape, axis)


def pack(block):
    turned = dot_nt(one_hot(iota((HALF, HALF), 0) == iota((HALF, HALF), 1)), block[0:384])
    tiles = [turned[:, 128 * j : 128 * j + 128] for j in range(3)]
    ends = jnp.concatenate([tile[96:100] for tile in tiles] + [jnp.zeros((4, 128), jnp.float32)], axis=0)
    return jnp.concatenate([tile[0:96].astype(jnp.bfloat16) for tile in tiles] + [ends.astype(jnp.bfloat16)], axis=0)


def weight_tiles(block):
    ends = block[288:304].astype(jnp.float32)
    none = jnp.zeros((12, 128), jnp.float32)
    ends = [jnp.concatenate([ends[4 * j : 4 * j + 4], none], axis=0).astype(jnp.bfloat16) for j in range(3)]
    rows = [jnp.concatenate([block[96 * j : 96 * j + 96] for j in range(3)], axis=1), jnp.concatenate(ends, axis=1)]
    return jnp.concatenate(rows + [jnp.zeros((16, 384), jnp.bfloat16)], axis=0), block[304:320]


def wrap(v, n):
    return jnp.where(v >= n, v - n, v)


def split(v):
    high = jnp.where(v >= 2, 1, 0)
    return high, v - 2 * high


def dot(a, b):
    return jnp.dot(a, b, preferred_element_type=jnp.float32)


def dot_nt(a, b):
    return lax.dot_general(a, b, (((1,), (1,)), ((), ())), preferred_element_type=jnp.float32)


def kernel(
    x_hbm, w0_hbm, w1_hbm, w2_hbm, w3_hbm, trow_ref, out_ref,
    x_ref, w_ref, packed, load_sem, weights, xs, acc, acc_rest, squares, hid, hid_rest, staged, first_sum, staged_sum, second_sum, mine,
    pick, squeeze, outbox, inbox,
    lane_send, lane_recv, ring_send, ring_recv, sib_send, sib_recv,
    gather_send, extra_send, pass_send, gather_recv, rest_recv, one_send, one_recv, two_send, two_recv, route_send, route_recv,
):
    x, dp, mp = lax.axis_index("section"), lax.axis_index("dp"), lax.axis_index("mp")
    z, yh, yl, c = dp // 2, dp % 2, mp // 2, mp % 2
    y = yh * 2 + yl
    group = x * 4 + mp

    def at(xx, zz, yy, cc):
        high, low = split(yy)
        return {"section": xx, "dp": zz * 2 + high, "mp": low * 2 + cc}

    above, below = wrap(z + 1, NZ), wrap(z + NZ - 1, NZ)
    up, down = at(x, above, y, c), at(x, below, y, c)
    sibling = at(x, z, y, 1 - c)
    lane_y, lane_c = c * 2 + yl, yh
    lane, lane_sibling = at(x, z, lane_y, lane_c), at(x, z, lane_y, 1 - lane_c)
    lane_up, lane_down = at(x, above, lane_y, lane_c), at(x, below, lane_y, lane_c)

    barrier = pltpu.get_barrier_semaphore()

    for i in range(1, 32):
        device = at(wrap(x + i // 8, 4), z, wrap(y + (i // 2) % 4, 4), wrap(c + i % 2, 2))
        pl.semaphore_signal(barrier, inc=1, device_id=device, device_id_type=MESH)
    for device in (up, down, lane_up, lane_down):
        pl.semaphore_signal(barrier, inc=1, device_id=device, device_id_type=MESH)

    loads = [pltpu.make_async_copy(x_hbm, x_ref, load_sem.at[4])]
    loads += [
        pltpu.make_async_copy(ref, w_ref.at[m], load_sem.at[m]) for m, ref in enumerate((w0_hbm, w1_hbm, w2_hbm, w3_hbm))
    ]
    for load in loads:
        load.start()

    def prepare(m):
        loads[1 + m].wait()
        packed[m, 0:304] = pack(w_ref[m])
        packed[m, 304:320] = jnp.zeros((16, 128), jnp.bfloat16)
        packed[m, 304:320, 0:HALF] = w_ref[m, 384:400]

    prepare(0)
    prepare(1)
    pl.semaphore_wait(barrier, 35)

    def landed(ref, sem):
        pltpu.make_async_copy(ref, ref, sem).wait()

    def slot(m, zz, cc):
        return weights.at[m, zz * 2 + cc]

    def piece(m, zz, cc, ch):
        return weights.at[m, zz * 2 + cc, pl.ds(ch * CHUNK, CHUNK)]

    def up_copy(m, zz, ch):
        return remote(piece(m, zz, c, ch), piece(m, zz, c, ch), ring_send, ring_recv.at[m, zz, ch], up)

    def down_copy(m, zz, ch):
        return remote(piece(m, zz, c, ch), piece(m, zz, c, ch), ring_send, ring_recv.at[m, zz, ch], down)

    def sib_copy(m, zz):
        return remote(slot(m, zz, c), slot(m, zz, c), sib_send, sib_recv.at[m], sibling)

    def lane_copy(m):
        return remote(packed.at[m], slot(m, z, lane_c), lane_send, lane_recv.at[m], lane)

    def ring_start(m):
        for ch in range(CHUNKS):
            src = packed.at[m, pl.ds(ch * CHUNK, CHUNK)]
            for device in (lane_up, lane_down):
                remote(src, piece(m, z, lane_c, ch), ring_send, ring_recv.at[m, z, ch], device).start()
        remote(packed.at[m], slot(m, z, lane_c), sib_send, sib_recv.at[m], lane_sibling).start()

        @pl.when(yh != c)
        def _():
            lane_copy(m).start()

        @pl.when(yh == c)
        def _():
            weights[m, z * 2 + c] = packed[m]

    def weights_wait(m):
        landed(weights.at[m, pl.ds(0, NZ)], sib_recv.at[m])

        @pl.when(yh != c)
        def _():
            landed(weights.at[m, 0], lane_recv.at[m])

    def ring_tick(m, s):
        a, b = wrap(z + NZ - s, NZ), wrap(z + s, NZ)
        for ch in range(CHUNKS):
            up_copy(m, a, ch).wait_recv()

            @pl.when((s < 7) | ((s == 7) & (m % 2 == 0)))
            def _(ch=ch):
                up_copy(m, a, ch).start()

            @pl.when(s < 8)
            def _(ch=ch):
                down_copy(m, b, ch).wait_recv()

            @pl.when((s < 7) | ((s == 7) & (m % 2 == 1)))
            def _(ch=ch):
                down_copy(m, b, ch).start()

    def sib_tick(m, s):
        sib_copy(m, wrap(z + NZ - s, NZ)).start()

        @pl.when(s < 8)
        def _():
            sib_copy(m, wrap(z + s, NZ)).start()

    def ticks(low, high, which=range(4)):
        def body(t, _):
            for m in which:
                if OFFSETS[m] and low <= OFFSETS[m] + 1 <= high:

                    @pl.when(t == OFFSETS[m] + 1)
                    def _(m=m):
                        ring_start(m)

            for step in (ring_tick, sib_tick):
                for m in which:
                    s = t - OFFSETS[m]
                    if low - OFFSETS[m] > 8 or high - OFFSETS[m] < 1:
                        continue

                    @pl.when((s >= 1) & (s <= 8))
                    def _(step=step, m=m, s=s):
                        step(m, s)

            return 0

        lax.fori_loop(low, high + 1, body, 0)

    def gather_copy(part, i):
        return remote(
            mine.at[part], xs.at[part, group], gather_send if i else extra_send, gather_recv.at[part, (1 - c) * x + c * (4 + yl)],
            at(wrap(x + i * (1 - c), 4), z, wrap(y + i * c, 4), yh),
        )

    def pass_y_copy(part, i, j):
        g = wrap(x + i, 4) * 4 + yl * 2
        return remote(
            xs.at[part, g], xs.at[part, g], pass_send, rest_recv.at[part], at(x, z, wrap(y + j, 4), c)
        )

    def pass_x_copy(part, i, j):
        g = x * 4 + i * 2 + 1
        return remote(
            xs.at[part, g], xs.at[part, g], gather_send, rest_recv.at[part], at(wrap(x + j, 4), z, y, c)
        )

    def arrive(part, g, k):
        @pl.when((g != group) | (yh != c))
        def _():
            landed(xs.at[part, 0], gather_recv.at[part, k])

    def gather_start(part):
        for i in range(1, 4):
            gather_copy(part, i).start()

        @pl.when(c != yh)
        def _():
            gather_copy(part, 0).start()

        @pl.when(c == yh)
        def _():
            xs[part, group] = mine[part]

    def gather_pass(part):
        for i in range(4):

            @pl.when(c == yh)
            def _(i=i):
                arrive(part, wrap(x + i, 4) * 4 + yl * 2, wrap(x + i, 4))
                for j in range(1, 4):
                    pass_y_copy(part, i, j).start()

            if i < 2:
                arrive(part, x * 4 + i * 2 + 1, 4 + i)
                for j in range(1, 4):
                    pass_x_copy(part, i, j).start()

    def gather_rest(part):
        @pl.when(yh == c)
        def _():
            landed(xs.at[part, pl.ds(0, 10)], rest_recv.at[part])

        @pl.when(yh != c)
        def _():
            landed(xs.at[part, pl.ds(0, 14)], rest_recv.at[part])

    def begin_up():
        acc[...] = jnp.zeros_like(acc)
        acc_rest[...] = jnp.zeros_like(acc_rest)
        squares[...] = jnp.zeros_like(squares)

    def up_unit(layer, zz):
        m = 2 * layer
        first, second = weight_tiles(weights[m, zz * 2]), weight_tiles(weights[m, zz * 2 + 1])
        halves = xs[2 * layer, zz], xs[2 * layer + 1, zz]
        rows = jnp.concatenate(halves, axis=1)
        acc[...] += dot(rows, jnp.concatenate([first[0], second[0]], axis=0))
        acc_rest[...] += dot_nt(rows, jnp.concatenate([first[1], second[1]], axis=1))
        for half in halves:
            wide = half.astype(jnp.float32)
            squares[...] += wide * wide

    def end_up():
        scale = lax.rsqrt(jnp.sum(squares[...], axis=1, keepdims=True) * (1.0 / DV) + EPSILON)

        def act(v):
            v = v * scale
            return (0.5 * v * (1.0 + jnp.tanh(0.7978845608028654 * (v + 0.044715 * (v * v * v))))).astype(jnp.bfloat16)

        hid[...] = act(acc[...])
        hid_rest[...] = act(acc_rest[...])

    def one_place(gx, gy, gc):
        return (split(gx)[0], y) if gc == 0 else (2 + gy, x)

    def one_copy(part, gx, gy, gc):
        k, src = one_place(gx, gy, gc)
        return remote(
            staged.at[part, gx * 4 + gy * 2 + gc], first_sum.at[part, k, src], one_send, one_recv.at[part, k],
            at(x, z, c * 2 + gy, split(gx)[1]) if gc == 0 else at(gx, z, y, c),
        )

    def to_self(gx, gy, gc):
        return (c * 2 + gy == y) & (split(gx)[1] == c) if gc == 0 else gx == x

    def down_unit(part, gx, gy, gc):
        m, half = 2 * (part // 2) + 1, part % 2

        main, rest = weight_tiles(weights[m, (gx * 4 + gy * 2 + gc) * 2 + half])
        total = (dot_nt(hid[...], main) + dot(hid_rest[...], rest)).astype(jnp.bfloat16)

        @pl.when(to_self(gx, gy, gc))
        def _():
            k, src = one_place(gx, gy, gc)
            first_sum[part, k, src] = total

        @pl.when(jnp.logical_not(to_self(gx, gy, gc)))
        def _():
            staged[part, gx * 4 + gy * 2 + gc] = total
            one_copy(part, gx, gy, gc).start()

    def two_copy(part, k):
        if k < 2:
            device, src = at(2 * k + c, z, y, 0), x
        else:
            device, src = at(x, z, c * 2 + k - 2, 1), y
        return remote(
            staged_sum.at[part, k], second_sum.at[part, src], two_send, two_recv.at[part], device
        )

    def two_self(k):
        return (2 * k + c == x) & (c == 0) if k < 2 else (y == c * 2 + k - 2) & (c == 1)

    def collect(part):
        for k in (0, 2, 1, 3):
            if k < 2:

                @pl.when(yh == c)
                def _(k=k):
                    landed(first_sum.at[part, k, pl.ds(0, 3)], one_recv.at[part, k])

                @pl.when(yh != c)
                def _(k=k):
                    landed(first_sum.at[part, k], one_recv.at[part, k])
            else:
                landed(first_sum.at[part, k, pl.ds(0, 3)], one_recv.at[part, k])
            total = None
            for src in range(4):
                term = first_sum[part, k, src].astype(jnp.float32)
                total = term if total is None else total + term
            total = total.astype(jnp.bfloat16)

            @pl.when(two_self(k))
            def _(k=k, total=total):
                second_sum[part, x if k < 2 else y] = total

            @pl.when(jnp.logical_not(two_self(k)))
            def _(k=k, total=total):
                staged_sum[part, k] = total
                two_copy(part, k).start()

    def own_total(part):
        with_self = ((c == 0) & (split(x)[1] == 0)) | ((c == 1) & (yh == 1))

        @pl.when(with_self)
        def _():
            landed(second_sum.at[part, pl.ds(0, 3)], two_recv.at[part])

        @pl.when(jnp.logical_not(with_self))
        def _():
            landed(second_sum.at[part], two_recv.at[part])

        total = mine[part].astype(jnp.float32)
        for src in range(4):
            total = total + second_sum[part, src].astype(jnp.float32)
        return total.astype(jnp.bfloat16)

    def groups(run):
        def body(i, _):
            gx = wrap(x + i, 4)
            for j in range(4):
                run(gx, wrap(yl + j // 2, 2), j % 2)
            return 0

        lax.fori_loop(1, 5, body, 0)

    def units(run):
        def body(s, _):
            run(wrap(z + s, NZ))
            run(wrap(z + NZ - s, NZ))
            return 0

        run(z)
        lax.fori_loop(1, 8, body, 0)
        run(wrap(z + 8, NZ))

    def route_copy(half, d, s):
        return remote(
            outbox.at[half, d], inbox.at[half, s], route_send, route_recv.at[half], {"dp": d}
        )

    def route_start(half):
        outbox[half] = dot(pick[...], own_total(2 + half)).astype(jnp.bfloat16).reshape(32, SLOT, 128)

        def body(i, _):
            for far in (16 - i, 16 + i):
                d = wrap(dp + far, 32)
                route_copy(half, d, dp).start()
            return 0

        route_copy(half, wrap(dp + 16, 32), dp).start()
        lax.fori_loop(1, 16, body, 0)
        inbox[half, dp] = outbox[half, dp]

    ring_start(0)
    ring_start(1)
    loads[0].wait()
    rows = x_ref[...]
    for half in range(2):
        shape = (2 * HALF, 128)
        widen = one_hot((iota(shape, 0) == iota(shape, 1) + half * HALF) & (iota(shape, 1) < HALF))
        mine[half] = dot(rows, widen).astype(jnp.bfloat16)
        gather_start(half)
    prepare(2)
    prepare(3)
    begin_up()
    trow = trow_ref[...]
    named = jnp.where(iota((32, ROWS), 0) == trow, 1.0, 0.0)
    before = one_hot(iota((ROWS, ROWS), 0) < iota((ROWS, ROWS), 1))
    position = jnp.sum(named * dot(named.astype(jnp.bfloat16), before), axis=0, keepdims=True).astype(jnp.int32)
    pick[...] = one_hot(iota((32 * SLOT, ROWS), 0) == trow * SLOT + position)

    r, q = iota((32 * CAP, 32 * SLOT), 0), iota((32 * CAP, 32 * SLOT), 1)
    squeeze[...] = one_hot(((q & 15) < CAP) & (r == (q >> 4) * CAP + (q & 15)))
    ticks(1, 2)
    gather_pass(0)
    gather_pass(1)
    ticks(3, 8)
    gather_rest(0)
    gather_rest(1)
    weights_wait(0)
    units(functools.partial(up_unit, 0))
    end_up()
    weights_wait(1)
    groups(functools.partial(down_unit, 0))
    groups(functools.partial(down_unit, 1))
    begin_up()
    ticks(9, 10)
    collect(0)
    collect(1)
    ticks(11, 11)
    mine[2] = own_total(0)
    gather_start(2)
    mine[3] = own_total(1)
    gather_start(3)
    ticks(12, 12)
    gather_pass(2)
    gather_pass(3)
    ticks(13, LAST)
    gather_rest(2)
    gather_rest(3)
    weights_wait(2)
    units(functools.partial(up_unit, 1))
    end_up()
    weights_wait(3)
    groups(functools.partial(down_unit, 2))
    groups(functools.partial(down_unit, 3))
    collect(2)
    collect(3)
    route_start(0)
    route_start(1)

    landed(weights.at[:, pl.ds(0, 15)], ring_send)
    landed(weights.at[:, pl.ds(0, 16)], sib_send)
    landed(xs.at[:, pl.ds(0, 9)], gather_send)

    @pl.when(yh != c)
    def _():
        landed(weights.at[0, pl.ds(0, 4)], lane_send)
        landed(xs.at[:, 0], extra_send)
        landed(xs.at[:, pl.ds(0, 14)], one_send)

    @pl.when(yh == c)
    def _():
        landed(xs.at[:, pl.ds(0, 12)], pass_send)
        landed(xs.at[:, pl.ds(0, 12)], one_send)

    two_at_home = ((c == 0) & (split(x)[1] == 0)) | ((c == 1) & (yh == 1))

    @pl.when(two_at_home)
    def _():
        landed(staged_sum.at[:, pl.ds(0, 3)], two_send)

    @pl.when(jnp.logical_not(two_at_home))
    def _():
        landed(staged_sum, two_send)

    total = None
    for half in range(2):
        landed(inbox.at[half, pl.ds(0, 31)], route_recv.at[half])
        rows = dot(squeeze[...], inbox[half].reshape(32 * SLOT, 128)).astype(jnp.bfloat16)
        shape = (2 * HALF, 128)
        narrow = one_hot((iota(shape, 0) == iota(shape, 1) + half * HALF) & (iota(shape, 1) < HALF))
        term = dot_nt(narrow, rows)
        total = term if total is None else total + term
    out_ref[...] = total.astype(jnp.bfloat16)
    landed(inbox.at[:, pl.ds(0, 31)], route_send)


def on_device(patches, up_first, down_first, up_second, down_second, targets):
    bf16, dma = jnp.bfloat16, pltpu.SemaphoreType.DMA
    vmem, anywhere = pl.BlockSpec(memory_space=pltpu.VMEM), pl.BlockSpec(memory_space=pl.ANY)
    placed = pl.pallas_call(
        kernel,
        out_shape=jax.ShapeDtypeStruct((2 * HALF, 32 * CAP), bf16),
        in_specs=[anywhere] * 5 + [vmem],
        out_specs=vmem,
        scratch_shapes=[
            pltpu.VMEM((ROWS, 2 * HALF), bf16),
            pltpu.VMEM((4, 400, HALF), bf16),
            pltpu.VMEM((4, PACK, 128), bf16),
            dma((5,)),
            pltpu.VMEM((4, 32, PACK, 128), bf16),
            pltpu.VMEM((4, 16, ROWS, 128), bf16),
            pltpu.VMEM((ROWS, 384), jnp.float32),
            pltpu.VMEM((ROWS, 16), jnp.float32),
            pltpu.VMEM((ROWS, 128), jnp.float32),
            pltpu.VMEM((ROWS, 384), bf16),
            pltpu.VMEM((ROWS, 16), bf16),
            pltpu.VMEM((4, 16, ROWS, 128), bf16),
            pltpu.VMEM((4, 4, 4, ROWS, 128), bf16),
            pltpu.VMEM((4, 4, ROWS, 128), bf16),
            pltpu.VMEM((4, 4, ROWS, 128), bf16),
            pltpu.VMEM((4, ROWS, 128), bf16),
            pltpu.VMEM((32 * SLOT, ROWS), bf16),
            pltpu.VMEM((32 * CAP, 32 * SLOT), bf16),
            pltpu.VMEM((2, 32, SLOT, 128), bf16),
            pltpu.VMEM((2, 32, SLOT, 128), bf16),
            dma(()), dma((4,)),
            dma(()), dma((4, NZ, CHUNKS)),
            dma(()), dma((4,)),
            dma(()), dma(()), dma(()), dma((4, 6)), dma((4,)),
            dma(()), dma((4, 4)),
            dma(()), dma((4,)),
            dma(()), dma((2,)),
        ],
        compiler_params=pltpu.CompilerParams(
            collective_id=0, has_side_effects=True, vmem_limit_bytes=60 * 1024 * 1024
        ),
    )(patches, up_first.T, down_first, up_second.T, down_second, targets.reshape(1, ROWS))
    return placed.T


def solution(mesh):
    in_specs = (
        P("dp", ("section", "mp")),
        P("dp", ("section", "mp")),
        P(("section", "mp"), "dp"),
        P("dp", ("section", "mp")),
        P(("section", "mp"), "dp"),
        P("dp", None),
    )
    return jax.shard_map(
        on_device, mesh=mesh, in_specs=in_specs, out_specs=P("dp", ("section", "mp")), check_vma=False
    )
```
